512 devices in a mesh: seq: 32 (over y, x, core), section: 16 (over z).
Axes of the slice: x: 4, y: 4, z: 16, core: 2. Of those that a mesh axis runs over, the one named last changes fastest.
Arguments:
- slabs: bfloat16 [16, 6144, 2048], P('section', 'seq'), may hold values from -6 to 6
- fresh: bfloat16 [1, 6144, 2048], P(None, 'seq'), may hold values from -6 to 6
- norm_gain: bfloat16 [16, 2048], P('section'), may hold values from 0.099609375 to 1.8984375
- qkv_proj: bfloat16 [16, 3, 16, 128, 128], P('section'), may hold values from -8 to 8
- o_proj: bfloat16 [16, 16, 128, 128], P('section'), may hold values from -0.5 to 0.5
- offsets: int32 [16, 16], P('section'), may hold values from 0 to 15
Outputs:
- result: bfloat16 [16, 6144, 2048], P('section', 'seq')
The draws below stay inside these ranges and needn't reach their ends.
All inputs are finite; a program needn't handle non-finite values.
Results may differ from the reference program's by a relative error of at most 0.023.
The reference program's roundings to bfloat16 on the way (of `normed`, `weights`, `attended` and `output`) count: a program that leaves them out, or rounds other values in their place, can miss the bound.
Values may be sent and summed in bfloat16 or wider, within the bound.
No kernel may reach another device: no remote copies, remote signals or barrier semaphores. Data moves between devices by JAX's collectives and lax.ppermute only.
A program may use at most 64 MiB of HBM per device.

```python
import math
import jax
import jax.numpy as jnp
from jax import lax

HEADS = 16
HEAD_DIM = 128
SEG_DEV = 192
RATE = 16
TICKS = 2
WIDTH = 2048
TOKENS = 6144
N_SEQ = 32
N_SECTION = 16


def draw_qkv_proj(key, part):
    shape = (N_SECTION, 3, HEADS, HEAD_DIM, HEAD_DIM)
    base = jax.random.normal(jax.random.fold_in(key, 11), shape, jnp.float32)
    base = jnp.clip(base, -5.0, 5.0) / math.sqrt(HEAD_DIM)
    return base.astype(jnp.bfloat16)


def with_ends(array, stream_key, smallest, high):
    longest = array.shape.index(max(array.shape))
    spots = []
    for shift in (0, 1):
        where = [jax.random.randint(jax.random.fold_in(stream_key, axis), (), 0, length) for axis, length in enumerate(array.shape)]
        where[longest] = (where[longest] + shift) % array.shape[longest]
        spots.append(tuple(where))
    return array.at[spots[0]].set(smallest).at[spots[1]].set(high)


def block_levels(own_key, dims, pieces, smallest, high):
    def one(dim, blocks):
        steps = jax.random.uniform(jax.random.fold_in(jax.random.fold_in(own_key, 6), dim), (blocks,), jnp.float32, smallest / len(pieces), high / len(pieces))
        return jnp.repeat(jnp.exp(steps), dims[dim] // blocks).reshape((-1,) + (1,) * (len(dims) - dim - 1))

    level = one(*pieces[0])
    for cut in pieces[1:]:
        level = level * one(*cut)
    return level


def noise(key, dims, deviation, most, pieces=(), kind=jnp.bfloat16):
    entries = jax.random.normal(key, dims, jnp.float32) * deviation
    if len(pieces) > 0:
        entries = block_levels(key, dims, pieces, -0.22, 0.18) * entries
    return jnp.clip(entries, min=-most, max=most).astype(kind)


def setup_inputs(seed: int = 0) -> dict:
    streams_of = jax.random.split(jax.random.key(seed), 7)
    return {
        "slabs": noise(streams_of[0], (N_SECTION, TOKENS, WIDTH), 1.0, 6.0, ((0, 16), (1, 32))),
        "fresh": noise(streams_of[1], (TICKS - 1, TOKENS, WIDTH), 1.0, 6.0, ((1, 32),)),
        "norm_gain": jnp.clip(1.0 + 0.18 * jax.random.normal(streams_of[2], (N_SECTION, WIDTH), jnp.float32), 0.099609375, 1.8984375).astype(jnp.bfloat16),
        "qkv_proj": draw_qkv_proj(jax.random.fold_in(streams_of[6], 71), 0),
        "o_proj": noise(streams_of[4], (N_SECTION, HEADS, HEAD_DIM, HEAD_DIM), HEAD_DIM ** -0.5, 0.5, ((0, 16),)),
        "offsets": with_ends(jax.random.randint(streams_of[5], (N_SECTION, HEADS), 0, RATE), jax.random.fold_in(streams_of[5], 1), 0, RATE - 1).astype(jnp.int32),
    }


eps = 1e-06
neg_big = -1e+30

def rounded(values):
    return lax.optimization_barrier(values.astype(jnp.bfloat16)).astype(jnp.float32)

def attend(queries, keys, values, mask):
    scale = 1.0 / math.sqrt(queries.shape[-1])
    scores = jnp.einsum('qhd,khd->qhk', queries, keys) * scale
    scores = jnp.where(mask[:, None, :], scores, neg_big)
    top = lax.optimization_barrier(jnp.max(scores, axis=-1, keepdims=True))
    expo = jnp.exp(scores - top)
    total = lax.optimization_barrier(jnp.sum(expo, axis=-1))
    summed = jnp.einsum('qhk,khd->qhd', rounded(expo), values)
    return summed / total[:, :, None]

def layer(state, gain, qkv_weights, o_weights, offsets):
    widened = state.astype(jnp.float32)
    scaled = widened * lax.rsqrt(lax.optimization_barrier(jnp.mean(widened * widened, axis=-1, keepdims=True)) + eps)
    normed = rounded(scaled * gain.astype(jnp.float32)).reshape(TOKENS, HEADS, HEAD_DIM)
    weights = qkv_weights.astype(jnp.float32)
    query = rounded(jnp.einsum('shd,hde->she', normed, weights[0]))
    key = rounded(jnp.einsum('shd,hde->she', normed, weights[1]))
    value = rounded(jnp.einsum('shd,hde->she', normed, weights[2]))
    phase = (lax.broadcasted_iota(jnp.int32, (RATE, HEADS), 0) == offsets[None, :]).astype(jnp.float32)
    panel_rows = SEG_DEV // RATE

    def dilate(field):
        grouped = field.reshape(N_SEQ, panel_rows, RATE, HEADS, HEAD_DIM)
        return lax.optimization_barrier(jnp.sum(grouped * phase[None, None, :, :, None], axis=2))
    key_panels = dilate(key)
    value_panels = dilate(value)
    seg_query = query.reshape(N_SEQ, SEG_DEV, HEADS, HEAD_DIM)
    seg_key = key.reshape(N_SEQ, SEG_DEV, HEADS, HEAD_DIM)
    seg_value = value.reshape(N_SEQ, SEG_DEV, HEADS, HEAD_DIM)
    levels = (N_SEQ - 1).bit_length()
    causal = lax.broadcasted_iota(jnp.int32, (SEG_DEV, SEG_DEV), 0) >= lax.broadcasted_iota(jnp.int32, (SEG_DEV, SEG_DEV), 1)

    def one_segment(segment):
        keys = [seg_key[segment]]
        vals = [seg_value[segment]]
        masks = [causal]
        for level in range(levels):
            source = segment - (1 << level)
            picked = jnp.maximum(source, 0)
            keys.append(key_panels[picked])
            vals.append(value_panels[picked])
            masks.append(jnp.broadcast_to(source >= 0, (SEG_DEV, panel_rows)))
        return attend(seg_query[segment], jnp.concatenate(keys, axis=0), jnp.concatenate(vals, axis=0), jnp.concatenate(masks, axis=1))
    attended = lax.map(one_segment, jnp.arange(N_SEQ, dtype=jnp.int32))
    attended = rounded(attended.reshape(TOKENS, HEADS, HEAD_DIM))
    mixed = jnp.einsum('qhd,hde->qhe', attended, o_weights.astype(jnp.float32))
    return (widened + mixed.reshape(TOKENS, WIDTH)).astype(jnp.bfloat16)

def reference(slabs, fresh, norm_gain, qkv_proj, o_proj, offsets):
    state = slabs

    def run_section(items):
        return layer(items[0], items[1], items[2], items[3], items[4])
    output = state
    for tick in range(TICKS):
        output = lax.map(run_section, (state, norm_gain, qkv_proj, o_proj, offsets))
        if tick < TICKS - 1:
            state = jnp.concatenate([fresh[tick][None], output[:-1]], axis=0)
    return output
```

```python
import functools
import math

import jax
import jax.numpy as jnp
from jax import lax
from jax.experimental import pallas as pl
from jax.experimental.pallas import tpu as pltpu
from jax.sharding import PartitionSpec as P

RATE = 16
HEADS = 16
DIM = 128
PACK = 8
SLOTS = 5
PAD = 16

eps = 1e-06
neg_big = -1e30
f32 = jnp.float32
bf16 = jnp.bfloat16

SMEM = pl.BlockSpec(memory_space=pltpu.SMEM)
VMEM = pl.BlockSpec(memory_space=pltpu.VMEM)


def inverse_rms(squares, width):
    return lax.rsqrt(squares * (1.0 / width) + eps)


def pick_panel(wide_ref, inv_ref, gain_ref, offsets_ref, panel_ref):
    count = wide_ref.shape[1] // RATE
    for head in range(HEADS):
        cols = slice(head * DIM, (head + 1) * DIM)
        where = pl.ds(offsets_ref[head], count, stride=RATE)
        picked = wide_ref[head, where, :] * inv_ref[where, :] * gain_ref[:, cols].astype(f32)
        panel_ref[:, cols] = jnp.concatenate(
            [picked, jnp.zeros((PAD - count, DIM), f32)], axis=0
        ).astype(bf16)


def norm_kernel(offsets_ref, state_ref, gain_ref, panel_ref, inv_ref, ahead_ref, wide_ref):
    width = state_ref.shape[1]
    ahead_ref[:, :width] = gain_ref[...]
    lane = lax.broadcasted_iota(jnp.int32, (1, DIM), 1)
    phases = jnp.zeros((1, DIM), jnp.int32)
    for head in range(HEADS):
        phases = jnp.where(lane == head, offsets_ref[head], phases)
    ahead_ref[:, width:] = phases.astype(f32).astype(bf16)
    squares = None
    for head in range(HEADS):
        cols = slice(head * DIM, (head + 1) * DIM)
        values = state_ref[:, cols].astype(f32)
        wide_ref[head] = values
        squares = values * values if squares is None else squares + values * values
    inverse = inverse_rms(jnp.sum(squares, axis=-1, keepdims=True), width)
    inv_ref[...] = jnp.broadcast_to(inverse, inv_ref.shape)
    pick_panel(wide_ref, inv_ref, gain_ref, offsets_ref, panel_ref)


def norm_panel(offsets, state, gain):
    rows, width = state.shape
    return pl.pallas_call(
        norm_kernel,
        out_shape=(
            jax.ShapeDtypeStruct((PAD, width), bf16),
            jax.ShapeDtypeStruct((rows, DIM), f32),
            jax.ShapeDtypeStruct((1, width + DIM), bf16),
        ),
        in_specs=[SMEM, VMEM, VMEM],
        out_specs=(VMEM, VMEM, VMEM),
        scratch_shapes=[pltpu.VMEM((HEADS, rows, DIM), f32)],
        cost_estimate=pl.CostEstimate(flops=2000000, bytes_accessed=1000000, transcendentals=0),
        name="norm_panel",
    )(offsets, state, gain)


def prepare_attention(place, chip_ref, first_ref, second_ref, swapped_ref, bias_ref, packed_ref, count):
    rows = bias_ref.shape[0]
    keys = bias_ref.shape[1]
    core = lax.rem(place, 2)
    other = 1 - core
    slots = [
        jnp.where(core == 0, first_ref[1], chip_ref[0]),
        first_ref[core],
        second_ref[core],
        swapped_ref[other, 0],
        swapped_ref[other, 1],
    ]
    for slot, panel in enumerate(slots):
        packed_ref[slot * count : (slot + 1) * count, :] = panel[:count].astype(f32)
    packed_ref[SLOTS * count :, :] = jnp.zeros(
        (packed_ref.shape[0] - SLOTS * count, packed_ref.shape[1]), f32
    )
    even, odd = (1, 2, 4, 8, 16), (1, 8, 16, 2, 4)
    row = lax.broadcasted_iota(jnp.int32, (rows, keys), 0)
    col = lax.broadcasted_iota(jnp.int32, (rows, keys), 1)
    allowed = (col < rows) & (col <= row)
    for slot in range(SLOTS):
        distance = jnp.where(core == 0, even[slot], odd[slot])
        start = jnp.where(place >= distance, rows + slot * count, keys)
        allowed = allowed | ((col >= start) & (col < rows + (slot + 1) * count))
    bias_ref[...] = jnp.where(allowed, 0.0, neg_big).astype(f32)


def some_heads(states, inverse, gains, queries, keys, values, outs, panels, bias):
    scale = math.log2(math.e) / math.sqrt(DIM)
    wide = [state.astype(f32) for state in states]
    normed = [(w * inverse * gain.astype(f32)).astype(bf16) for w, gain in zip(wide, gains)]
    both = [jnp.concatenate([n, panel.astype(bf16)], axis=0) for n, panel in zip(normed, panels)]
    query = [jnp.dot(n, w, preferred_element_type=f32).astype(bf16) for n, w in zip(normed, queries)]
    pair = [
        jnp.dot(rows, jnp.concatenate([k, v], axis=1), preferred_element_type=f32).astype(bf16)
        for rows, k, v in zip(both, keys, values)
    ]
    scores = [
        lax.dot_general(q, p[:, :DIM], (((1,), (1,)), ((), ())), preferred_element_type=f32)
        for q, p in zip(query, pair)
    ]
    scores = [s * scale + bias for s in scores]
    expo = [jnp.exp2(s - jnp.max(s, axis=-1, keepdims=True)) for s in scores]
    total = [jnp.sum(e, axis=-1, keepdims=True) for e in expo]
    summed = [
        jnp.dot(e.astype(bf16), p[:, DIM:], preferred_element_type=f32) for e, p in zip(expo, pair)
    ]
    attended = [(m * (1.0 / t)).astype(bf16) for m, t in zip(summed, total)]
    mixed = [jnp.dot(a, w, preferred_element_type=f32) for a, w in zip(attended, outs)]
    return [(w + m).astype(bf16) for w, m in zip(wide, mixed)]


def first_kernel(
    place_ref, offsets_ref,
    state_ref, inv_ref, gain_ref, qkv_ref, o_ref, chip_ref, first_ref, second_ref, swapped_ref, gain_next_ref,
    out_ref, panel_ref,
    bias_ref, packed_ref, wide_ref, squares_ref, inv_next_ref,
):
    step = pl.program_id(0)
    rows = state_ref.shape[0]
    count = rows // RATE

    @pl.when(step == 0)
    def _():
        prepare_attention(
            place_ref[0], chip_ref, first_ref, second_ref, swapped_ref, bias_ref, packed_ref, count
        )

    inverse, bias = inv_ref[...], bias_ref[...]
    squares = jnp.zeros((rows, DIM), f32)
    local_cols = [slice(local * DIM, (local + 1) * DIM) for local in range(PACK)]
    there = [pl.ds(pl.multiple_of((step * PACK + local) * DIM, DIM), DIM) for local in range(PACK)]
    results = some_heads(
        [state_ref[:, cols] for cols in local_cols], inverse, [gain_ref[:, cols] for cols in local_cols],
        [qkv_ref[0, i] for i in range(PACK)], [qkv_ref[1, i] for i in range(PACK)], [qkv_ref[2, i] for i in range(PACK)],
        [o_ref[i] for i in range(PACK)], [packed_ref[:, at] for at in there], bias,
    )
    for local, result in enumerate(results):
        out_ref[:, local_cols[local]] = result
        values = result.astype(f32)
        wide_ref[step * PACK + local] = values
        squares = squares + values * values
    squares_ref[...] = jnp.where(step == 0, squares, squares_ref[...] + squares)

    @pl.when(step == pl.num_programs(0) - 1)
    def _():
        total = jnp.sum(squares_ref[...], axis=-1, keepdims=True)
        inv_next_ref[...] = jnp.broadcast_to(inverse_rms(total, HEADS * DIM), inv_next_ref.shape)
        pick_panel(wide_ref, inv_next_ref, gain_next_ref, offsets_ref, panel_ref)


def attention_specs(rows, width):
    return [
        pl.BlockSpec((1, PACK * DIM), lambda i: (0, i)),
        pl.BlockSpec((3, PACK, DIM, DIM), lambda i: (0, i, 0, 0)),
        pl.BlockSpec((PACK, DIM, DIM), lambda i: (i, 0, 0)),
        pl.BlockSpec((2, PAD, width), lambda i: (0, 0, 0)),
        pl.BlockSpec((2, PAD, width), lambda i: (0, 0, 0)),
        pl.BlockSpec((2, PAD, width), lambda i: (0, 0, 0)),
        pl.BlockSpec((2, 2, PAD, width), lambda i: (0, 0, 0, 0)),
    ]


def first_layer(place, offsets_next, state, inv, gain, qkv, o_weights, fetched, gain_next):
    rows, width = state.shape
    keys = 256
    return pl.pallas_call(
        first_kernel,
        grid=(HEADS // PACK,),
        out_shape=(
            jax.ShapeDtypeStruct((rows, width), bf16),
            jax.ShapeDtypeStruct((PAD, width), bf16),
        ),
        in_specs=[
            SMEM,
            SMEM,
            pl.BlockSpec((rows, PACK * DIM), lambda i: (0, i)),
            pl.BlockSpec((rows, DIM), lambda i: (0, 0)),
            *attention_specs(rows, width),
            pl.BlockSpec((1, width), lambda i: (0, 0)),
        ],
        out_specs=(
            pl.BlockSpec((rows, PACK * DIM), lambda i: (0, i)),
            pl.BlockSpec((PAD, width), lambda i: (0, 0)),
        ),
        scratch_shapes=[
            pltpu.VMEM((rows, keys), f32),
            pltpu.VMEM((keys - rows, width), f32),
            pltpu.VMEM((HEADS, rows, DIM), f32),
            pltpu.VMEM((rows, DIM), f32),
            pltpu.VMEM((rows, DIM), f32),
        ],
        compiler_params=pltpu.CompilerParams(vmem_limit_bytes=60 << 20),
        cost_estimate=pl.CostEstimate(flops=800000000, bytes_accessed=5000000, transcendentals=800000),
        name="first_layer",
    )(place, offsets_next, state, inv, gain, qkv, o_weights, *fetched, gain_next)


def last_kernel(
    place_ref, first_section_ref,
    moved_ref, fresh_ref, gain_ref, qkv_ref, o_ref, chip_ref, first_ref, second_ref, swapped_ref,
    out_ref,
    bias_ref, packed_ref, state_ref, inv_ref,
):
    step = pl.program_id(0)
    rows, width = moved_ref.shape
    count = rows // RATE

    @pl.when(step == 0)
    def _():
        prepare_attention(
            place_ref[0], chip_ref, first_ref, second_ref, swapped_ref, bias_ref, packed_ref, count
        )
        is_first = first_section_ref[0] == 1
        squares = None
        for head in range(HEADS):
            cols = slice(head * DIM, (head + 1) * DIM)
            values = jnp.where(is_first, fresh_ref[:, cols], moved_ref[:, cols])
            state_ref[:, cols] = values
            values = values.astype(f32)
            squares = values * values if squares is None else squares + values * values
        inverse = inverse_rms(jnp.sum(squares, axis=-1, keepdims=True), width)
        inv_ref[...] = jnp.broadcast_to(inverse, inv_ref.shape)

    inverse, bias = inv_ref[...], bias_ref[...]
    local_cols = [slice(local * DIM, (local + 1) * DIM) for local in range(PACK)]
    there = [pl.ds(pl.multiple_of((step * PACK + local) * DIM, DIM), DIM) for local in range(PACK)]
    results = some_heads(
        [state_ref[:, at] for at in there], inverse, [gain_ref[:, cols] for cols in local_cols],
        [qkv_ref[0, i] for i in range(PACK)], [qkv_ref[1, i] for i in range(PACK)], [qkv_ref[2, i] for i in range(PACK)],
        [o_ref[i] for i in range(PACK)], [packed_ref[:, at] for at in there], bias,
    )
    for local, result in enumerate(results):
        out_ref[:, local_cols[local]] = result


def last_layer(place, first_section, moved, fresh, gain, qkv, o_weights, fetched):
    rows, width = moved.shape
    keys = 256
    return pl.pallas_call(
        last_kernel,
        grid=(HEADS // PACK,),
        out_shape=jax.ShapeDtypeStruct((rows, width), bf16),
        in_specs=[
            SMEM,
            SMEM,
            pl.BlockSpec((rows, width), lambda i: (0, 0)),
            pl.BlockSpec((rows, width), lambda i: (0, 0)),
            *attention_specs(rows, width),
        ],
        out_specs=pl.BlockSpec((rows, PACK * DIM), lambda i: (0, i)),
        scratch_shapes=[
            pltpu.VMEM((rows, keys), f32),
            pltpu.VMEM((keys - rows, width), f32),
            pltpu.VMEM((rows, width), bf16),
            pltpu.VMEM((rows, DIM), f32),
        ],
        compiler_params=pltpu.CompilerParams(vmem_limit_bytes=60 << 20),
        cost_estimate=pl.CostEstimate(flops=800000000, bytes_accessed=5000000, transcendentals=800000),
        name="last_layer",
    )(place, first_section, moved, fresh, gain, qkv, o_weights, *fetched)


def shifted(value, axis, steps):
    count = lax.axis_size(axis)
    first, last = max(0, -steps), min(count, count - steps)
    return lax.ppermute(value, axis, [(source, source + steps) for source in range(first, last)])


def by_core(value, even_steps, odd_steps):
    chips = lax.axis_size("seq") // 2
    pairs = [(2 * c, 2 * (c + even_steps)) for c in range(chips - even_steps)]
    pairs += [(2 * c + 1, 2 * (c + odd_steps) + 1) for c in range(chips - odd_steps)]
    return lax.ppermute(value, "seq", pairs)


def fetch(panel, core):
    count = lax.axis_size("seq")
    cores = [[chip, chip + 1] for chip in range(0, count, 2)]
    chip = lax.all_gather(panel, "seq", axis=0, axis_index_groups=cores)
    first = by_core(chip, 1, 4)
    second = by_core(chip, 2, 8)
    mine = jnp.stack(
        [
            lax.dynamic_index_in_dim(first, 1 - core, 0, keepdims=False),
            lax.dynamic_index_in_dim(second, 1 - core, 0, keepdims=False),
        ]
    )
    swapped = lax.all_gather(mine, "seq", axis=0, axis_index_groups=cores)
    return chip, first, second, swapped


def on_device(slabs, fresh, norm_gain, qkv_proj, o_proj, offsets):
    place = lax.axis_index("seq").astype(jnp.int32)
    section = lax.axis_index("section")
    core = lax.rem(place, 2)
    here = place.reshape(1)
    is_first = (section == 0).astype(jnp.int32)
    state, entering = slabs[0], fresh[0]
    gain, qkv, o_weights = norm_gain, qkv_proj[0], o_proj[0]

    panel, inv, ahead = norm_panel(offsets[0], state, gain)
    fetched = fetch(panel, core)
    ahead = shifted(ahead, "section", -1)
    gain_next = ahead[:, : HEADS * DIM]
    offsets_next = ahead[0, HEADS * DIM : HEADS * DIM + HEADS].astype(jnp.int32)
    output, panel_next = first_layer(
        here, offsets_next, state, inv, gain, qkv, o_weights, fetched, gain_next
    )
    entering_panel, _, _ = norm_panel(offsets[0], entering, gain)
    moved_panel = shifted(panel_next, "section", 1)
    moved = shifted(output, "section", 1)
    panel = jnp.where(is_first == 1, entering_panel, moved_panel)
    fetched = fetch(panel, core)
    result = last_layer(here, is_first.reshape(1), moved, entering, gain, qkv, o_weights, fetched)
    return result[None]


def solution(mesh):
    in_specs = (
        P("section", "seq", None),
        P(None, "seq", None),
        P("section", None),
        P("section", None, None, None, None),
        P("section", None, None, None),
        P("section", None),
    )
    out_specs = P("section", "seq", None)
    return jax.shard_map(
        on_device, mesh=mesh, in_specs=in_specs, out_specs=out_specs, check_vma=False
    )
```

```python
import functools
import math

import jax
import jax.numpy as jnp
from jax import lax
from jax.experimental import pallas as pl
from jax.experimental.pallas import tpu as pltpu
from jax.sharding import PartitionSpec as P

RATE = 16
HEADS = 16
DIM = 128
PACK = 8
SLOTS = 5
KEYS = 256
PAD = 16

eps = 1e-06
neg_big = -1e30
f32 = jnp.float32
bf16 = jnp.bfloat16

SMEM = pl.BlockSpec(memory_space=pltpu.SMEM)
VMEM = pl.BlockSpec(memory_space=pltpu.VMEM)
ANY = pl.BlockSpec(memory_space=pl.ANY)


def inverse_rms(squares, width):
    return lax.rsqrt(squares * (1.0 / width) + eps)


def pick_panel(wide_ref, inv_ref, gain_ref, offsets_ref, panel_ref):
    count = wide_ref.shape[1] // RATE
    for head in range(HEADS):
        cols = slice(head * DIM, (head + 1) * DIM)
        where = pl.ds(offsets_ref[head], count, stride=RATE)
        picked = wide_ref[head, where, :] * inv_ref[where, :] * gain_ref[:, cols].astype(f32)
        panel_ref[:, cols] = jnp.concatenate(
            [picked, jnp.zeros((PAD - count, DIM), f32)], axis=0
        ).astype(bf16)


def norm_kernel(offsets_ref, state_ref, gain_ref, panel_ref, inv_ref, ahead_ref, wide_ref):
    width = state_ref.shape[1]
    ahead_ref[:, :width] = gain_ref[...]
    lane = lax.broadcasted_iota(jnp.int32, (1, DIM), 1)
    phases = jnp.zeros((1, DIM), jnp.int32)
    for head in range(HEADS):
        phases = jnp.where(lane == head, offsets_ref[head], phases)
    ahead_ref[:, width:] = phases.astype(f32).astype(bf16)
    squares = None
    for head in range(HEADS):
        cols = slice(head * DIM, (head + 1) * DIM)
        values = state_ref[:, cols].astype(f32)
        wide_ref[head] = values
        squares = values * values if squares is None else squares + values * values
    inverse = inverse_rms(jnp.sum(squares, axis=-1, keepdims=True), width)
    inv_ref[...] = jnp.broadcast_to(inverse, inv_ref.shape)
    pick_panel(wide_ref, inv_ref, gain_ref, offsets_ref, panel_ref)


def norm_panel(offsets, state, gain):
    rows, width = state.shape
    return pl.pallas_call(
        norm_kernel,
        out_shape=(
            jax.ShapeDtypeStruct((PAD, width), bf16),
            jax.ShapeDtypeStruct((rows, DIM), f32),
            jax.ShapeDtypeStruct((1, width + DIM), bf16),
        ),
        in_specs=[SMEM, VMEM, VMEM],
        out_specs=(VMEM, VMEM, VMEM),
        scratch_shapes=[pltpu.VMEM((HEADS, rows, DIM), f32)],
        cost_estimate=pl.CostEstimate(flops=2000000, bytes_accessed=1000000, transcendentals=0),
        name="norm_panel",
    )(offsets, state, gain)


def pack_panels(core, chip_ref, first_ref, second_ref, swapped_ref, packed_ref, count):
    width = packed_ref.shape[1]
    other = 1 - core
    slots = [
        jnp.where(core == 0, first_ref[1], chip_ref[0]),
        first_ref[core],
        second_ref[core],
        swapped_ref[other, 0],
        swapped_ref[other, 1],
    ]
    for slot, panel in enumerate(slots):
        packed_ref[slot * count : (slot + 1) * count, :] = panel[:count].astype(f32)
    packed_ref[SLOTS * count :, :] = jnp.zeros((packed_ref.shape[0] - SLOTS * count, width), f32)


def write_bias(place, bias_ref, count):
    rows, keys = bias_ref.shape
    core = lax.rem(place, 2)
    even, odd = (1, 2, 4, 8, 16), (1, 8, 16, 2, 4)
    row = lax.broadcasted_iota(jnp.int32, (rows, keys), 0)
    col = lax.broadcasted_iota(jnp.int32, (rows, keys), 1)
    allowed = (col < rows) & (col <= row)
    for slot in range(SLOTS):
        distance = jnp.where(core == 0, even[slot], odd[slot])
        start = jnp.where(place >= distance, rows + slot * count, keys)
        allowed = allowed | ((col >= start) & (col < rows + (slot + 1) * count))
    bias_ref[...] = jnp.where(allowed, 0.0, neg_big).astype(f32)


def entering_kernel(place_ref, is_first_ref, offsets_ref, fresh_ref, gain_ref, panel_ref, bias_ref, state_ref, wide_ref, inv_ref, sem):
    write_bias(place_ref[0], bias_ref, wide_ref.shape[1] // RATE)

    @pl.when(is_first_ref[0] == 1)
    def _():
        copy = pltpu.make_async_copy(fresh_ref, state_ref, sem)
        copy.start()
        copy.wait()
        squares = None
        for head in range(HEADS):
            values = state_ref[:, head * DIM : (head + 1) * DIM].astype(f32)
            wide_ref[head] = values
            squares = values * values if squares is None else squares + values * values
        inverse = inverse_rms(jnp.sum(squares, axis=-1, keepdims=True), HEADS * DIM)
        inv_ref[...] = jnp.broadcast_to(inverse, inv_ref.shape)
        pick_panel(wide_ref, inv_ref, gain_ref, offsets_ref, panel_ref)

    @pl.when(is_first_ref[0] == 0)
    def _():
        panel_ref[...] = jnp.zeros(panel_ref.shape, panel_ref.dtype)


def entering_panel(place, is_first, offsets, fresh, gain):
    rows, width = fresh.shape
    return pl.pallas_call(
        entering_kernel,
        out_shape=(
            jax.ShapeDtypeStruct((PAD, width), bf16),
            jax.ShapeDtypeStruct((rows, KEYS), f32),
        ),
        in_specs=[SMEM, SMEM, SMEM, ANY, VMEM],
        out_specs=(VMEM, VMEM),
        scratch_shapes=[
            pltpu.VMEM((rows, width), bf16),
            pltpu.VMEM((HEADS, rows, DIM), f32),
            pltpu.VMEM((rows, DIM), f32),
            pltpu.SemaphoreType.DMA,
        ],
        compiler_params=pltpu.CompilerParams(vmem_limit_bytes=60 << 20),
        cost_estimate=pl.CostEstimate(flops=2000000, bytes_accessed=1000000, transcendentals=0),
        name="entering_panel",
    )(place, is_first, offsets, fresh, gain)


def some_heads(states, inverse, gains, queries, keys, values, outs, panels, bias):
    scale = math.log2(math.e) / math.sqrt(DIM)
    wide = [state.astype(f32) for state in states]
    normed = [(w * inverse * gain.astype(f32)).astype(bf16) for w, gain in zip(wide, gains)]
    both = [jnp.concatenate([n, panel.astype(bf16)], axis=0) for n, panel in zip(normed, panels)]
    query = [jnp.dot(n, w, preferred_element_type=f32).astype(bf16) for n, w in zip(normed, queries)]
    pair = [
        jnp.dot(rows, jnp.concatenate([k, v], axis=1), preferred_element_type=f32).astype(bf16)
        for rows, k, v in zip(both, keys, values)
    ]
    scores = [
        lax.dot_general(q, p[:, :DIM], (((1,), (1,)), ((), ())), preferred_element_type=f32)
        for q, p in zip(query, pair)
    ]
    scores = [s * scale + bias for s in scores]
    expo = [jnp.exp2(s - jnp.max(s, axis=-1, keepdims=True)) for s in scores]
    total = [jnp.sum(e, axis=-1, keepdims=True) for e in expo]
    summed = [
        jnp.dot(e.astype(bf16), p[:, DIM:], preferred_element_type=f32) for e, p in zip(expo, pair)
    ]
    attended = [(m * (1.0 / t)).astype(bf16) for m, t in zip(summed, total)]
    mixed = [jnp.dot(a, w, preferred_element_type=f32) for a, w in zip(attended, outs)]
    return [(w + m).astype(bf16) for w, m in zip(wide, mixed)]


def first_kernel(
    place_ref, offsets_ref,
    state_ref, inv_ref, bias_ref, gain_ref, qkv_ref, o_ref, chip_ref, first_ref, second_ref, swapped_ref, gain_next_ref,
    out_ref, panel_ref,
    packed_ref, wide_ref, squares_ref, inv_next_ref,
):
    step = pl.program_id(0)
    rows = state_ref.shape[0]
    count = rows // RATE

    @pl.when(step == 0)
    def _():
        pack_panels(
            lax.rem(place_ref[0], 2), chip_ref, first_ref, second_ref, swapped_ref, packed_ref, count
        )

    inverse, bias = inv_ref[...], bias_ref[...]
    squares = jnp.zeros((rows, DIM), f32)
    local_cols = [slice(local * DIM, (local + 1) * DIM) for local in range(PACK)]
    there = [pl.ds(pl.multiple_of((step * PACK + local) * DIM, DIM), DIM) for local in range(PACK)]
    results = some_heads(
        [state_ref[:, cols] for cols in local_cols], inverse, [gain_ref[:, cols] for cols in local_cols],
        [qkv_ref[0, i] for i in range(PACK)], [qkv_ref[1, i] for i in range(PACK)], [qkv_ref[2, i] for i in range(PACK)],
        [o_ref[i] for i in range(PACK)], [packed_ref[:, at] for at in there], bias,
    )
    for local, result in enumerate(results):
        out_ref[:, local_cols[local]] = result
        values = result.astype(f32)
        wide_ref[step * PACK + local] = values
        squares = squares + values * values
    squares_ref[...] = jnp.where(step == 0, squares, squares_ref[...] + squares)

    @pl.when(step == pl.num_programs(0) - 1)
    def _():
        total = jnp.sum(squares_ref[...], axis=-1, keepdims=True)
        inv_next_ref[...] = jnp.broadcast_to(inverse_rms(total, HEADS * DIM), inv_next_ref.shape)
        pick_panel(wide_ref, inv_next_ref, gain_next_ref, offsets_ref, panel_ref)


def attention_specs(rows, width):
    return [
        pl.BlockSpec((1, PACK * DIM), lambda i: (0, i)),
        pl.BlockSpec((3, PACK, DIM, DIM), lambda i: (0, i, 0, 0)),
        pl.BlockSpec((PACK, DIM, DIM), lambda i: (i, 0, 0)),
        pl.BlockSpec((2, PAD, width), lambda i: (0, 0, 0)),
        pl.BlockSpec((2, PAD, width), lambda i: (0, 0, 0)),
        pl.BlockSpec((2, PAD, width), lambda i: (0, 0, 0)),
        pl.BlockSpec((2, 2, PAD, width), lambda i: (0, 0, 0, 0)),
    ]


def first_layer(place, offsets_next, state, inv, gain, bias, qkv, o_weights, fetched, gain_next):
    rows, width = state.shape
    return pl.pallas_call(
        first_kernel,
        grid=(HEADS // PACK,),
        out_shape=(
            jax.ShapeDtypeStruct((rows, width), bf16),
            jax.ShapeDtypeStruct((PAD, width), bf16),
        ),
        in_specs=[
            SMEM,
            SMEM,
            pl.BlockSpec((rows, PACK * DIM), lambda i: (0, i)),
            pl.BlockSpec((rows, DIM), lambda i: (0, 0)),
            pl.BlockSpec((rows, KEYS), lambda i: (0, 0)),
            *attention_specs(rows, width),
            pl.BlockSpec((1, width), lambda i: (0, 0)),
        ],
        out_specs=(
            pl.BlockSpec((rows, PACK * DIM), lambda i: (0, i)),
            pl.BlockSpec((PAD, width), lambda i: (0, 0)),
        ),
        scratch_shapes=[
            pltpu.VMEM((KEYS - rows, width), f32),
            pltpu.VMEM((HEADS, rows, DIM), f32),
            pltpu.VMEM((rows, DIM), f32),
            pltpu.VMEM((rows, DIM), f32),
        ],
        compiler_params=pltpu.CompilerParams(vmem_limit_bytes=60 << 20),
        cost_estimate=pl.CostEstimate(flops=800000000, bytes_accessed=5000000, transcendentals=800000),
        name="first_layer",
    )(place, offsets_next, state, inv, bias, gain, qkv, o_weights, *fetched, gain_next)


def last_kernel(
    place_ref, is_first_ref,
    moved_ref, fresh_ref, bias_ref, gain_ref, qkv_ref, o_ref, chip_ref, first_ref, second_ref, swapped_ref,
    out_ref,
    packed_ref, state_ref, inv_ref, sem,
):
    step = pl.program_id(0)
    rows, width = moved_ref.shape
    count = rows // RATE

    @pl.when(step == 0)
    def _():
        pack_panels(
            lax.rem(place_ref[0], 2), chip_ref, first_ref, second_ref, swapped_ref, packed_ref, count
        )

        @pl.when(is_first_ref[0] == 1)
        def _():
            copy = pltpu.make_async_copy(fresh_ref, state_ref, sem)
            copy.start()
            copy.wait()

        @pl.when(is_first_ref[0] == 0)
        def _():
            state_ref[...] = moved_ref[...]

        squares = None
        for head in range(HEADS):
            values = state_ref[:, head * DIM : (head + 1) * DIM].astype(f32)
            squares = values * values if squares is None else squares + values * values
        inverse = inverse_rms(jnp.sum(squares, axis=-1, keepdims=True), width)
        inv_ref[...] = jnp.broadcast_to(inverse, inv_ref.shape)

    inverse, bias = inv_ref[...], bias_ref[...]
    local_cols = [slice(local * DIM, (local + 1) * DIM) for local in range(PACK)]
    there = [pl.ds(pl.multiple_of((step * PACK + local) * DIM, DIM), DIM) for local in range(PACK)]
    results = some_heads(
        [state_ref[:, at] for at in there], inverse, [gain_ref[:, cols] for cols in local_cols],
        [qkv_ref[0, i] for i in range(PACK)], [qkv_ref[1, i] for i in range(PACK)], [qkv_ref[2, i] for i in range(PACK)],
        [o_ref[i] for i in range(PACK)], [packed_ref[:, at] for at in there], bias,
    )
    for local, result in enumerate(results):
        out_ref[:, local_cols[local]] = result


def last_layer(place, is_first, moved, fresh, gain, bias, qkv, o_weights, fetched):
    rows, width = moved.shape
    return pl.pallas_call(
        last_kernel,
        grid=(HEADS // PACK,),
        out_shape=jax.ShapeDtypeStruct((rows, width), bf16),
        in_specs=[
            SMEM,
            SMEM,
            pl.BlockSpec((rows, width), lambda i: (0, 0)),
            ANY,
            pl.BlockSpec((rows, KEYS), lambda i: (0, 0)),
            *attention_specs(rows, width),
        ],
        out_specs=pl.BlockSpec((rows, PACK * DIM), lambda i: (0, i)),
        scratch_shapes=[
            pltpu.VMEM((KEYS - rows, width), f32),
            pltpu.VMEM((rows, width), bf16),
            pltpu.VMEM((rows, DIM), f32),
            pltpu.SemaphoreType.DMA,
        ],
        compiler_params=pltpu.CompilerParams(vmem_limit_bytes=48 << 20),
        cost_estimate=pl.CostEstimate(flops=800000000, bytes_accessed=5000000, transcendentals=800000),
        name="last_layer",
    )(place, is_first, moved, fresh, bias, gain, qkv, o_weights, *fetched)


def shifted(value, axis, steps):
    count = lax.axis_size(axis)
    first, last = max(0, -steps), min(count, count - steps)
    return lax.ppermute(value, axis, [(source, source + steps) for source in range(first, last)])


def by_core(value, even_steps, odd_steps):
    chips = lax.axis_size("seq") // 2
    pairs = [(2 * c, 2 * (c + even_steps)) for c in range(chips - even_steps)]
    pairs += [(2 * c + 1, 2 * (c + odd_steps) + 1) for c in range(chips - odd_steps)]
    return lax.ppermute(value, "seq", pairs)


def fetch(panel, core):
    count = lax.axis_size("seq")
    cores = [[chip, chip + 1] for chip in range(0, count, 2)]
    chip = lax.all_gather(panel, "seq", axis=0, axis_index_groups=cores)
    first = by_core(chip, 1, 4)
    second = by_core(chip, 2, 8)
    mine = jnp.stack(
        [
            lax.dynamic_index_in_dim(first, 1 - core, 0, keepdims=False),
            lax.dynamic_index_in_dim(second, 1 - core, 0, keepdims=False),
        ]
    )
    swapped = lax.all_gather(mine, "seq", axis=0, axis_index_groups=cores)
    return chip, first, second, swapped


def on_device(slabs, fresh, norm_gain, qkv_proj, o_proj, offsets):
    place = lax.axis_index("seq").astype(jnp.int32)
    section = lax.axis_index("section")
    core = lax.rem(place, 2)
    here = place.reshape(1)
    is_first = (section == 0).astype(jnp.int32)
    state, entering = slabs[0], fresh[0]
    gain, qkv, o_weights = norm_gain, qkv_proj[0], o_proj[0]

    panel, inv, ahead = norm_panel(offsets[0], state, gain)
    fetched = fetch(panel, core)
    ahead = shifted(ahead, "section", -1)
    gain_next = ahead[:, : HEADS * DIM]
    offsets_next = ahead[0, HEADS * DIM : HEADS * DIM + HEADS].astype(jnp.int32)
    own_panel, bias = entering_panel(here, is_first.reshape(1), offsets[0], entering, gain)
    output, panel_next = first_layer(
        here, offsets_next, state, inv, gain, bias, qkv, o_weights, fetched, gain_next
    )
    moved_panel = shifted(panel_next, "section", 1)
    moved = shifted(output, "section", 1)
    panel = jnp.where(is_first == 1, own_panel, moved_panel)
    fetched = lax.fori_loop(
        0, 1 + jnp.minimum(offsets[0, 0], 0), lambda _, previous: fetch(panel, core), fetched
    )
    result = last_layer(here, is_first.reshape(1), moved, entering, gain, bias, qkv, o_weights, fetched)
    return result[None]


def solution(mesh):
    in_specs = (
        P("section", "seq", None),
        P(None, "seq", None),
        P("section", None),
        P("section", None, None, None, None),
        P("section", None, None, None),
        P("section", None),
    )
    out_specs = P("section", "seq", None)
    return jax.shard_map(
        on_device, mesh=mesh, in_specs=in_specs, out_specs=out_specs, check_vma=False
    )
```

```python
import functools
import math

import jax
import jax.numpy as jnp
from jax import lax
from jax.experimental import pallas as pl
from jax.experimental.pallas import tpu as pltpu
from jax.sharding import PartitionSpec as P

RATE = 16
HEADS = 16
DIM = 128
PACK = 8
SLOTS = 5
KEYS = 256
PAD = 16

eps = 1e-06
neg_big = -1e30
f32 = jnp.float32
bf16 = jnp.bfloat16

SMEM = pl.BlockSpec(memory_space=pltpu.SMEM)
VMEM = pl.BlockSpec(memory_space=pltpu.VMEM)
ANY = pl.BlockSpec(memory_space=pl.ANY)


def inverse_rms(squares, width):
    return lax.rsqrt(squares * (1.0 / width) + eps)


def pick_panel(wide_ref, inv_ref, gain_ref, offset_of, panel_ref):
    count = wide_ref.shape[1] // RATE
    for head in range(HEADS):
        cols = slice(head * DIM, (head + 1) * DIM)
        where = pl.ds(offset_of(head), count, stride=RATE)
        picked = wide_ref[head, where, :] * inv_ref[where, :] * gain_ref[:, cols].astype(f32)
        panel_ref[:, cols] = jnp.concatenate(
            [picked, jnp.zeros((PAD - count, DIM), f32)], axis=0
        ).astype(bf16)


def norm_kernel(offsets_ref, state_ref, gain_ref, panel_ref, inv_ref, ahead_ref, wide_ref):
    width = state_ref.shape[1]
    ahead_ref[:, :width] = gain_ref[...]
    lane = lax.broadcasted_iota(jnp.int32, (1, DIM), 1)
    phases = jnp.zeros((1, DIM), jnp.int32)
    for head in range(HEADS):
        phases = jnp.where(lane == head, offsets_ref[head], phases)
    ahead_ref[:, width:] = phases.astype(f32).astype(bf16)
    squares = None
    for head in range(HEADS):
        cols = slice(head * DIM, (head + 1) * DIM)
        values = state_ref[:, cols].astype(f32)
        wide_ref[head] = values
        squares = values * values if squares is None else squares + values * values
    inverse = inverse_rms(jnp.sum(squares, axis=-1, keepdims=True), width)
    inv_ref[...] = jnp.broadcast_to(inverse, inv_ref.shape)
    pick_panel(wide_ref, inv_ref, gain_ref, lambda head: offsets_ref[head], panel_ref)


def norm_panel(offsets, state, gain):
    rows, width = state.shape
    return pl.pallas_call(
        norm_kernel,
        out_shape=(
            jax.ShapeDtypeStruct((PAD, width), bf16),
            jax.ShapeDtypeStruct((rows, DIM), f32),
            jax.ShapeDtypeStruct((1, width + DIM), bf16),
        ),
        in_specs=[SMEM, VMEM, VMEM],
        out_specs=(VMEM, VMEM, VMEM),
        scratch_shapes=[pltpu.VMEM((HEADS, rows, DIM), f32)],
        cost_estimate=pl.CostEstimate(flops=2000000, bytes_accessed=1000000, transcendentals=0),
        name="norm_panel",
    )(offsets, state, gain)


def pack_panels(core, chip_ref, first_ref, second_ref, swapped_ref, packed_ref, count):
    width = packed_ref.shape[1]
    other = 1 - core
    slots = [
        jnp.where(core == 0, first_ref[1], chip_ref[0]),
        first_ref[core],
        second_ref[core],
        swapped_ref[other, 0],
        swapped_ref[other, 1],
    ]
    for slot, panel in enumerate(slots):
        packed_ref[slot * count : (slot + 1) * count, :] = panel[:count].astype(f32)
    packed_ref[SLOTS * count :, :] = jnp.zeros((packed_ref.shape[0] - SLOTS * count, width), f32)


def write_bias(place, bias_ref, count):
    rows, keys = bias_ref.shape
    core = lax.rem(place, 2)
    even, odd = (1, 2, 4, 8, 16), (1, 8, 16, 2, 4)
    row = lax.broadcasted_iota(jnp.int32, (rows, keys), 0)
    col = lax.broadcasted_iota(jnp.int32, (rows, keys), 1)
    allowed = (col < rows) & (col <= row)
    for slot in range(SLOTS):
        distance = jnp.where(core == 0, even[slot], odd[slot])
        start = jnp.where(place >= distance, rows + slot * count, keys)
        allowed = allowed | ((col >= start) & (col < rows + (slot + 1) * count))
    bias_ref[...] = jnp.where(allowed, 0.0, neg_big).astype(f32)


def entering_kernel(place_ref, is_first_ref, offsets_ref, fresh_ref, gain_ref, panel_ref, bias_ref, state_ref, wide_ref, inv_ref, sem):
    write_bias(place_ref[0], bias_ref, wide_ref.shape[1] // RATE)

    @pl.when(is_first_ref[0] == 1)
    def _():
        copy = pltpu.make_async_copy(fresh_ref, state_ref, sem)
        copy.start()
        copy.wait()
        squares = None
        for head in range(HEADS):
            values = state_ref[:, head * DIM : (head + 1) * DIM].astype(f32)
            wide_ref[head] = values
            squares = values * values if squares is None else squares + values * values
        inverse = inverse_rms(jnp.sum(squares, axis=-1, keepdims=True), HEADS * DIM)
        inv_ref[...] = jnp.broadcast_to(inverse, inv_ref.shape)
        pick_panel(wide_ref, inv_ref, gain_ref, lambda head: offsets_ref[head], panel_ref)

    @pl.when(is_first_ref[0] == 0)
    def _():
        panel_ref[...] = jnp.zeros(panel_ref.shape, panel_ref.dtype)


def entering_panel(place, is_first, offsets, fresh, gain):
    rows, width = fresh.shape
    return pl.pallas_call(
        entering_kernel,
        out_shape=(
            jax.ShapeDtypeStruct((PAD, width), bf16),
            jax.ShapeDtypeStruct((rows, KEYS), f32),
        ),
        in_specs=[SMEM, SMEM, SMEM, ANY, VMEM],
        out_specs=(VMEM, VMEM),
        scratch_shapes=[
            pltpu.VMEM((rows, width), bf16),
            pltpu.VMEM((HEADS, rows, DIM), f32),
            pltpu.VMEM((rows, DIM), f32),
            pltpu.SemaphoreType.DMA,
        ],
        compiler_params=pltpu.CompilerParams(vmem_limit_bytes=60 << 20),
        cost_estimate=pl.CostEstimate(flops=2000000, bytes_accessed=1000000, transcendentals=0),
        name="entering_panel",
    )(place, is_first, offsets, fresh, gain)


def some_heads(states, inverse, gains, queries, keys, values, outs, panels, bias):
    scale = math.log2(math.e) / math.sqrt(DIM)
    wide = [state.astype(f32) for state in states]
    normed = [(w * inverse * gain.astype(f32)).astype(bf16) for w, gain in zip(wide, gains)]
    both = [jnp.concatenate([n, panel.astype(bf16)], axis=0) for n, panel in zip(normed, panels)]
    query = [jnp.dot(n, w, preferred_element_type=f32).astype(bf16) for n, w in zip(normed, queries)]
    pair = [
        jnp.dot(rows, jnp.concatenate([k, v], axis=1), preferred_element_type=f32).astype(bf16)
        for rows, k, v in zip(both, keys, values)
    ]
    scores = [
        lax.dot_general(q, p[:, :DIM], (((1,), (1,)), ((), ())), preferred_element_type=f32)
        for q, p in zip(query, pair)
    ]
    scores = [s * scale + bias for s in scores]
    expo = [jnp.exp2(s - jnp.max(s, axis=-1, keepdims=True)) for s in scores]
    total = [jnp.sum(e, axis=-1, keepdims=True) for e in expo]
    summed = [
        jnp.dot(e.astype(bf16), p[:, DIM:], preferred_element_type=f32) for e, p in zip(expo, pair)
    ]
    attended = [(m * (1.0 / t)).astype(bf16) for m, t in zip(summed, total)]
    mixed = [jnp.dot(a, w, preferred_element_type=f32) for a, w in zip(attended, outs)]
    return [(w + m).astype(bf16) for w, m in zip(wide, mixed)]


def first_kernel(
    place_ref,
    state_ref, inv_ref, bias_ref, gain_ref, qkv_ref, o_ref, chip_ref, first_ref, second_ref, swapped_ref, gain_next_ref,
    out_ref, panel_ref,
    packed_ref, wide_ref, squares_ref, inv_next_ref, phases_ref, phases_smem, sem,
):
    step = pl.program_id(0)
    rows = state_ref.shape[0]
    count = rows // RATE

    @pl.when(step == 0)
    def _():
        phases_ref[...] = gain_next_ref[:, HEADS * DIM :].astype(f32).astype(jnp.int32)
        pltpu.make_async_copy(phases_ref, phases_smem, sem).start()
        pack_panels(
            lax.rem(place_ref[0], 2), chip_ref, first_ref, second_ref, swapped_ref, packed_ref, count
        )

    inverse, bias = inv_ref[...], bias_ref[...]
    squares = jnp.zeros((rows, DIM), f32)
    local_cols = [slice(local * DIM, (local + 1) * DIM) for local in range(PACK)]
    there = [pl.ds(pl.multiple_of((step * PACK + local) * DIM, DIM), DIM) for local in range(PACK)]
    results = some_heads(
        [state_ref[:, cols] for cols in local_cols], inverse, [gain_ref[:, cols] for cols in local_cols],
        [qkv_ref[0, i] for i in range(PACK)], [qkv_ref[1, i] for i in range(PACK)], [qkv_ref[2, i] for i in range(PACK)],
        [o_ref[i] for i in range(PACK)], [packed_ref[:, at] for at in there], bias,
    )
    for local, result in enumerate(results):
        out_ref[:, local_cols[local]] = result
        values = result.astype(f32)
        wide_ref[step * PACK + local] = values
        squares = squares + values * values
    squares_ref[...] = jnp.where(step == 0, squares, squares_ref[...] + squares)

    @pl.when(step == pl.num_programs(0) - 1)
    def _():
        total = jnp.sum(squares_ref[...], axis=-1, keepdims=True)
        inv_next_ref[...] = jnp.broadcast_to(inverse_rms(total, HEADS * DIM), inv_next_ref.shape)
        pltpu.make_async_copy(phases_ref, phases_smem, sem).wait()
        pick_panel(wide_ref, inv_next_ref, gain_next_ref, lambda head: phases_smem[0, head], panel_ref)


def attention_specs(rows, width):
    return [
        pl.BlockSpec((1, PACK * DIM), lambda i: (0, i)),
        pl.BlockSpec((3, PACK, DIM, DIM), lambda i: (0, i, 0, 0)),
        pl.BlockSpec((PACK, DIM, DIM), lambda i: (i, 0, 0)),
        pl.BlockSpec((2, PAD, width), lambda i: (0, 0, 0)),
        pl.BlockSpec((2, PAD, width), lambda i: (0, 0, 0)),
        pl.BlockSpec((2, PAD, width), lambda i: (0, 0, 0)),
        pl.BlockSpec((2, 2, PAD, width), lambda i: (0, 0, 0, 0)),
    ]


def first_layer(place, state, inv, gain, bias, qkv, o_weights, fetched, gain_next):
    rows, width = state.shape
    return pl.pallas_call(
        first_kernel,
        grid=(HEADS // PACK,),
        out_shape=(
            jax.ShapeDtypeStruct((rows, width), bf16),
            jax.ShapeDtypeStruct((PAD, width), bf16),
        ),
        in_specs=[
            SMEM,
            pl.BlockSpec((rows, PACK * DIM), lambda i: (0, i)),
            pl.BlockSpec((rows, DIM), lambda i: (0, 0)),
            pl.BlockSpec((rows, KEYS), lambda i: (0, 0)),
            *attention_specs(rows, width),
            pl.BlockSpec((1, width + DIM), lambda i: (0, 0)),
        ],
        out_specs=(
            pl.BlockSpec((rows, PACK * DIM), lambda i: (0, i)),
            pl.BlockSpec((PAD, width), lambda i: (0, 0)),
        ),
        scratch_shapes=[
            pltpu.VMEM((KEYS - rows, width), f32),
            pltpu.VMEM((HEADS, rows, DIM), f32),
            pltpu.VMEM((rows, DIM), f32),
            pltpu.VMEM((rows, DIM), f32),
            pltpu.VMEM((1, DIM), jnp.int32),
            pltpu.SMEM((1, DIM), jnp.int32),
            pltpu.SemaphoreType.DMA,
        ],
        compiler_params=pltpu.CompilerParams(vmem_limit_bytes=60 << 20),
        cost_estimate=pl.CostEstimate(flops=800000000, bytes_accessed=5000000, transcendentals=800000),
        name="first_layer",
    )(place, state, inv, bias, gain, qkv, o_weights, *fetched, gain_next)


def last_kernel(
    place_ref, is_first_ref,
    moved_ref, fresh_ref, bias_ref, gain_ref, qkv_ref, o_ref, chip_ref, first_ref, second_ref, swapped_ref,
    out_ref,
    packed_ref, state_ref, out_buf, sem, out_sems,
):
    rows, width = moved_ref.shape

    @pl.when(is_first_ref[0] == 1)
    def _():
        copy = pltpu.make_async_copy(fresh_ref, state_ref, sem)
        copy.start()
        copy.wait()

    @pl.when(is_first_ref[0] == 0)
    def _():
        state_ref[...] = moved_ref[...]

    pack_panels(
        lax.rem(place_ref[0], 2), chip_ref, first_ref, second_ref, swapped_ref, packed_ref, rows // RATE
    )
    squares = None
    for head in range(HEADS):
        values = state_ref[:, head * DIM : (head + 1) * DIM].astype(f32)
        squares = values * values if squares is None else squares + values * values
    inverse = jnp.broadcast_to(
        inverse_rms(jnp.sum(squares, axis=-1, keepdims=True), width), (rows, DIM)
    )
    bias = bias_ref[...]
    outs = []
    for group in range(HEADS // PACK):
        heads = range(group * PACK, (group + 1) * PACK)
        cols = [slice(head * DIM, (head + 1) * DIM) for head in heads]
        results = some_heads(
            [state_ref[:, c] for c in cols], inverse, [gain_ref[:, c] for c in cols],
            [qkv_ref[0, h] for h in heads], [qkv_ref[1, h] for h in heads], [qkv_ref[2, h] for h in heads],
            [o_ref[h] for h in heads], [packed_ref[:, c] for c in cols], bias,
        )
        for c, result in zip(cols, results):
            out_buf[:, c] = result
        block = slice(group * PACK * DIM, (group + 1) * PACK * DIM)
        out = pltpu.make_async_copy(out_buf.at[:, block], out_ref.at[:, block], out_sems.at[group])
        out.start()
        outs.append(out)
    for out in outs:
        out.wait()


def last_layer(place, is_first, moved, fresh, gain, bias, qkv, o_weights, fetched):
    rows, width = moved.shape
    return pl.pallas_call(
        last_kernel,
        out_shape=jax.ShapeDtypeStruct((rows, width), bf16),
        in_specs=[SMEM, SMEM, VMEM, ANY, *[VMEM] * 8],
        out_specs=ANY,
        scratch_shapes=[
            pltpu.VMEM((KEYS - rows, width), f32),
            pltpu.VMEM((rows, width), bf16),
            pltpu.VMEM((rows, width), bf16),
            pltpu.SemaphoreType.DMA,
            pltpu.SemaphoreType.DMA((HEADS // PACK,)),
        ],
        compiler_params=pltpu.CompilerParams(vmem_limit_bytes=48 << 20),
        cost_estimate=pl.CostEstimate(flops=800000000, bytes_accessed=5000000, transcendentals=800000),
        name="last_layer",
    )(place, is_first, moved, fresh, bias, gain, qkv, o_weights, *fetched)


def shifted(value, axis, steps):
    count = lax.axis_size(axis)
    first, last = max(0, -steps), min(count, count - steps)
    return lax.ppermute(value, axis, [(source, source + steps) for source in range(first, last)])


def by_core(value, even_steps, odd_steps):
    chips = lax.axis_size("seq") // 2
    pairs = [(2 * c, 2 * (c + even_steps)) for c in range(chips - even_steps)]
    pairs += [(2 * c + 1, 2 * (c + odd_steps) + 1) for c in range(chips - odd_steps)]
    return lax.ppermute(value, "seq", pairs)


def fetch(panel, core, beside=None):
    count = lax.axis_size("seq")
    cores = [[chip, chip + 1] for chip in range(0, count, 2)]
    chip = lax.all_gather(panel, "seq", axis=0, axis_index_groups=cores)
    first = by_core(chip, 1, 4)
    second = by_core(chip, 2, 8)
    mine = jnp.stack(
        [
            lax.dynamic_index_in_dim(first, 1 - core, 0, keepdims=False),
            lax.dynamic_index_in_dim(second, 1 - core, 0, keepdims=False),
        ]
    )
    if beside is not None:
        mine, beside = lax.optimization_barrier((mine, beside))
    swapped = lax.all_gather(mine, "seq", axis=0, axis_index_groups=cores)
    return (chip, first, second, swapped) if beside is None else ((chip, first, second, swapped), beside)


def on_device(slabs, fresh, norm_gain, qkv_proj, o_proj, offsets):
    place = lax.axis_index("seq").astype(jnp.int32)
    section = lax.axis_index("section")
    core = lax.rem(place, 2)
    here = place.reshape(1)
    is_first = (section == 0).astype(jnp.int32)
    state, entering = slabs[0], fresh[0]
    gain, qkv, o_weights = norm_gain, qkv_proj[0], o_proj[0]

    panel, inv, ahead = norm_panel(offsets[0], state, gain)
    fetched, ahead = fetch(panel, core, shifted(ahead, "section", -1))
    own_panel, bias = entering_panel(here, is_first.reshape(1), offsets[0], entering, gain)
    output, panel_next = first_layer(
        here, state, inv, gain, bias, qkv, o_weights, fetched, ahead
    )
    moved_panel = shifted(panel_next, "section", 1)
    moved = shifted(output, "section", 1)
    panel = jnp.where(is_first == 1, own_panel, moved_panel)
    fetched = lax.fori_loop(
        0, 1 + jnp.minimum(offsets[0, 0], 0), lambda _, previous: fetch(panel, core), fetched
    )
    result = last_layer(here, is_first.reshape(1), moved, entering, gain, bias, qkv, o_weights, fetched)
    return result[None]


def solution(mesh):
    in_specs = (
        P("section", "seq", None),
        P(None, "seq", None),
        P("section", None),
        P("section", None, None, None, None),
        P("section", None, None, None),
        P("section", None),
    )
    out_specs = P("section", "seq", None)
    return jax.shard_map(
        on_device, mesh=mesh, in_specs=in_specs, out_specs=out_specs, check_vma=False
    )
```

```python
import functools
import math

import jax
import jax.numpy as jnp
from jax import lax
from jax.experimental import pallas as pl
from jax.experimental.pallas import tpu as pltpu
from jax.sharding import PartitionSpec as P

RATE = 16
HEADS = 16
DIM = 128
PACK = 8
SLOTS = 5
KEYS = 256
PIECES = 4
PAD = 16

eps = 1e-06
neg_big = -1e30
f32 = jnp.float32
bf16 = jnp.bfloat16

SMEM = pl.BlockSpec(memory_space=pltpu.SMEM)
VMEM = pl.BlockSpec(memory_space=pltpu.VMEM)
ANY = pl.BlockSpec(memory_space=pl.ANY)


def inverse_rms(squares, width):
    return lax.rsqrt(squares * (1.0 / width) + eps)


def pick_panel(wide_ref, inv_ref, gain_ref, offset_of, panel_ref):
    count = wide_ref.shape[1] // RATE
    for head in range(HEADS):
        cols = slice(head * DIM, (head + 1) * DIM)
        where = pl.ds(offset_of(head), count, stride=RATE)
        picked = wide_ref[head, where, :] * inv_ref[where, :] * gain_ref[:, cols].astype(f32)
        panel_ref[:, cols] = jnp.concatenate(
            [picked, jnp.zeros((PAD - count, DIM), f32)], axis=0
        ).astype(bf16)


def norm_kernel(offsets_ref, state_ref, gain_ref, panel_ref, inv_ref, ahead_ref, wide_ref):
    width = state_ref.shape[1]
    ahead_ref[:, :width] = gain_ref[...]
    lane = lax.broadcasted_iota(jnp.int32, (1, DIM), 1)
    phases = jnp.zeros((1, DIM), jnp.int32)
    for head in range(HEADS):
        phases = jnp.where(lane == head, offsets_ref[head], phases)
    ahead_ref[:, width:] = phases.astype(f32).astype(bf16)
    squares = None
    for head in range(HEADS):
        cols = slice(head * DIM, (head + 1) * DIM)
        values = state_ref[:, cols].astype(f32)
        wide_ref[head] = values
        squares = values * values if squares is None else squares + values * values
    inverse = inverse_rms(jnp.sum(squares, axis=-1, keepdims=True), width)
    inv_ref[...] = jnp.broadcast_to(inverse, inv_ref.shape)
    pick_panel(wide_ref, inv_ref, gain_ref, lambda head: offsets_ref[head], panel_ref)


def norm_panel(offsets, state, gain):
    rows, width = state.shape
    return pl.pallas_call(
        norm_kernel,
        out_shape=(
            jax.ShapeDtypeStruct((PAD, width), bf16),
            jax.ShapeDtypeStruct((rows, DIM), f32),
            jax.ShapeDtypeStruct((1, width + DIM), bf16),
        ),
        in_specs=[SMEM, VMEM, VMEM],
        out_specs=(VMEM, VMEM, VMEM),
        scratch_shapes=[pltpu.VMEM((HEADS, rows, DIM), f32)],
        cost_estimate=pl.CostEstimate(flops=2000000, bytes_accessed=1000000, transcendentals=0),
        name="norm_panel",
    )(offsets, state, gain)


def pack_panels(core, chip_ref, first_ref, second_ref, swapped_ref, packed_ref, count):
    width = packed_ref.shape[1]
    other = 1 - core
    slots = [
        jnp.where(core == 0, first_ref[1], chip_ref[0]),
        first_ref[core],
        second_ref[core],
        swapped_ref[other, 0],
        swapped_ref[other, 1],
    ]
    for slot, panel in enumerate(slots):
        packed_ref[slot * count : (slot + 1) * count, :] = panel[:count].astype(f32)
    packed_ref[SLOTS * count :, :] = jnp.zeros((packed_ref.shape[0] - SLOTS * count, width), f32)


def fetch_slots(core, chip_ref, first_ref, second_ref, swapped_ref, slots_ref, sems):
    other = 1 - core
    sources = [first_ref.at[core], second_ref.at[core], swapped_ref.at[other, 0], swapped_ref.at[other, 1]]
    copies = [
        pltpu.make_async_copy(source, slots_ref.at[1 + slot], sems.at[1 + slot])
        for slot, source in enumerate(sources)
    ]
    for copy in copies:
        copy.start()

    @pl.when(core == 0)
    def _():
        pltpu.make_async_copy(first_ref.at[1], slots_ref.at[0], sems.at[0]).start()

    @pl.when(core == 1)
    def _():
        pltpu.make_async_copy(chip_ref.at[0], slots_ref.at[0], sems.at[0]).start()

    return [pltpu.make_async_copy(chip_ref.at[0], slots_ref.at[0], sems.at[0]), *copies]


def pack_slots(slots_ref, packed_ref, count):
    width = packed_ref.shape[1]
    for slot in range(SLOTS):
        packed_ref[slot * count : (slot + 1) * count, :] = slots_ref[slot][:count].astype(f32)
    packed_ref[SLOTS * count :, :] = jnp.zeros((packed_ref.shape[0] - SLOTS * count, width), f32)


def write_bias(place, bias_ref, count):
    rows, keys = bias_ref.shape
    core = lax.rem(place, 2)
    even, odd = (1, 2, 4, 8, 16), (1, 8, 16, 2, 4)
    row = lax.broadcasted_iota(jnp.int32, (rows, keys), 0)
    col = lax.broadcasted_iota(jnp.int32, (rows, keys), 1)
    allowed = (col < rows) & (col <= row)
    for slot in range(SLOTS):
        distance = jnp.where(core == 0, even[slot], odd[slot])
        start = jnp.where(place >= distance, rows + slot * count, keys)
        allowed = allowed | ((col >= start) & (col < rows + (slot + 1) * count))
    bias_ref[...] = jnp.where(allowed, 0.0, neg_big).astype(f32)


def entering_kernel(place_ref, is_first_ref, offsets_ref, fresh_ref, gain_ref, panel_ref, bias_ref, state_ref, wide_ref, inv_ref, sem):
    write_bias(place_ref[0], bias_ref, wide_ref.shape[1] // RATE)

    @pl.when(is_first_ref[0] == 1)
    def _():
        copy = pltpu.make_async_copy(fresh_ref, state_ref, sem)
        copy.start()
        copy.wait()
        squares = None
        for head in range(HEADS):
            values = state_ref[:, head * DIM : (head + 1) * DIM].astype(f32)
            wide_ref[head] = values
            squares = values * values if squares is None else squares + values * values
        inverse = inverse_rms(jnp.sum(squares, axis=-1, keepdims=True), HEADS * DIM)
        inv_ref[...] = jnp.broadcast_to(inverse, inv_ref.shape)
        pick_panel(wide_ref, inv_ref, gain_ref, lambda head: offsets_ref[head], panel_ref)

    @pl.when(is_first_ref[0] == 0)
    def _():
        panel_ref[...] = jnp.zeros(panel_ref.shape, panel_ref.dtype)


def entering_panel(place, is_first, offsets, fresh, gain):
    rows, width = fresh.shape
    return pl.pallas_call(
        entering_kernel,
        out_shape=(
            jax.ShapeDtypeStruct((PAD, width), bf16),
            jax.ShapeDtypeStruct((rows, KEYS), f32),
        ),
        in_specs=[SMEM, SMEM, SMEM, ANY, VMEM],
        out_specs=(VMEM, VMEM),
        scratch_shapes=[
            pltpu.VMEM((rows, width), bf16),
            pltpu.VMEM((HEADS, rows, DIM), f32),
            pltpu.VMEM((rows, DIM), f32),
            pltpu.SemaphoreType.DMA,
        ],
        compiler_params=pltpu.CompilerParams(vmem_limit_bytes=60 << 20),
        cost_estimate=pl.CostEstimate(flops=2000000, bytes_accessed=1000000, transcendentals=0),
        name="entering_panel",
    )(place, is_first, offsets, fresh, gain)


def some_heads(states, inverse, gains, queries, keys, values, outs, panels, bias):
    scale = math.log2(math.e) / math.sqrt(DIM)
    wide = [state.astype(f32) for state in states]
    normed = [(w * inverse * gain.astype(f32)).astype(bf16) for w, gain in zip(wide, gains)]
    both = [jnp.concatenate([n, panel.astype(bf16)], axis=0) for n, panel in zip(normed, panels)]
    query = [jnp.dot(n, w, preferred_element_type=f32).astype(bf16) for n, w in zip(normed, queries)]
    pair = [
        jnp.dot(rows, jnp.concatenate([k, v], axis=1), preferred_element_type=f32).astype(bf16)
        for rows, k, v in zip(both, keys, values)
    ]
    scores = [
        lax.dot_general(q, p[:, :DIM], (((1,), (1,)), ((), ())), preferred_element_type=f32)
        for q, p in zip(query, pair)
    ]
    scores = [s * scale + bias for s in scores]
    expo = [jnp.exp2(s - jnp.max(s, axis=-1, keepdims=True)) for s in scores]
    total = [jnp.sum(e, axis=-1, keepdims=True) for e in expo]
    summed = [
        jnp.dot(e.astype(bf16), p[:, DIM:], preferred_element_type=f32) for e, p in zip(expo, pair)
    ]
    attended = [(m * (1.0 / t)).astype(bf16) for m, t in zip(summed, total)]
    mixed = [jnp.dot(a, w, preferred_element_type=f32) for a, w in zip(attended, outs)]
    return [(w + m).astype(bf16) for w, m in zip(wide, mixed)]


def first_kernel(
    place_ref,
    state_ref, inv_ref, bias_ref, gain_ref, qkv_ref, o_ref, chip_ref, first_ref, second_ref, swapped_ref, gain_next_ref,
    out_ref, panel_ref,
    packed_ref, wide_ref, squares_ref, inv_next_ref, phases_ref, phases_smem, sem,
):
    step = pl.program_id(0)
    rows = state_ref.shape[0]
    count = rows // RATE

    @pl.when(step == 0)
    def _():
        phases_ref[...] = gain_next_ref[:, HEADS * DIM :].astype(f32).astype(jnp.int32)
        pltpu.make_async_copy(phases_ref, phases_smem, sem).start()
        pack_panels(
            lax.rem(place_ref[0], 2), chip_ref, first_ref, second_ref, swapped_ref, packed_ref, count
        )

    inverse, bias = inv_ref[...], bias_ref[...]
    squares = jnp.zeros((rows, DIM), f32)
    local_cols = [slice(local * DIM, (local + 1) * DIM) for local in range(PACK)]
    there = [pl.ds(pl.multiple_of((step * PACK + local) * DIM, DIM), DIM) for local in range(PACK)]
    results = some_heads(
        [state_ref[:, cols] for cols in local_cols], inverse, [gain_ref[:, cols] for cols in local_cols],
        [qkv_ref[0, i] for i in range(PACK)], [qkv_ref[1, i] for i in range(PACK)], [qkv_ref[2, i] for i in range(PACK)],
        [o_ref[i] for i in range(PACK)], [packed_ref[:, at] for at in there], bias,
    )
    for local, result in enumerate(results):
        out_ref[:, local_cols[local]] = result
        values = result.astype(f32)
        wide_ref[step * PACK + local] = values
        squares = squares + values * values
    squares_ref[...] = jnp.where(step == 0, squares, squares_ref[...] + squares)

    @pl.when(step == pl.num_programs(0) - 1)
    def _():
        total = jnp.sum(squares_ref[...], axis=-1, keepdims=True)
        inv_next_ref[...] = jnp.broadcast_to(inverse_rms(total, HEADS * DIM), inv_next_ref.shape)
        pltpu.make_async_copy(phases_ref, phases_smem, sem).wait()
        pick_panel(wide_ref, inv_next_ref, gain_next_ref, lambda head: phases_smem[0, head], panel_ref)


def attention_specs(rows, width):
    return [
        pl.BlockSpec((1, PACK * DIM), lambda i: (0, i)),
        pl.BlockSpec((3, PACK, DIM, DIM), lambda i: (0, i, 0, 0)),
        pl.BlockSpec((PACK, DIM, DIM), lambda i: (i, 0, 0)),
        pl.BlockSpec((2, PAD, width), lambda i: (0, 0, 0)),
        pl.BlockSpec((2, PAD, width), lambda i: (0, 0, 0)),
        pl.BlockSpec((2, PAD, width), lambda i: (0, 0, 0)),
        pl.BlockSpec((2, 2, PAD, width), lambda i: (0, 0, 0, 0)),
    ]


def first_layer(place, state, inv, gain, bias, qkv, o_weights, fetched, gain_next):
    rows, width = state.shape
    return pl.pallas_call(
        first_kernel,
        grid=(HEADS // PACK,),
        out_shape=(
            jax.ShapeDtypeStruct((rows, width), bf16),
            jax.ShapeDtypeStruct((PAD, width), bf16),
        ),
        in_specs=[
            SMEM,
            pl.BlockSpec((rows, PACK * DIM), lambda i: (0, i)),
            pl.BlockSpec((rows, DIM), lambda i: (0, 0)),
            pl.BlockSpec((rows, KEYS), lambda i: (0, 0)),
            *attention_specs(rows, width),
            pl.BlockSpec((1, width + DIM), lambda i: (0, 0)),
        ],
        out_specs=(
            pl.BlockSpec((rows, PACK * DIM), lambda i: (0, i)),
            pl.BlockSpec((PAD, width), lambda i: (0, 0)),
        ),
        scratch_shapes=[
            pltpu.VMEM((KEYS - rows, width), f32),
            pltpu.VMEM((HEADS, rows, DIM), f32),
            pltpu.VMEM((rows, DIM), f32),
            pltpu.VMEM((rows, DIM), f32),
            pltpu.VMEM((1, DIM), jnp.int32),
            pltpu.SMEM((1, DIM), jnp.int32),
            pltpu.SemaphoreType.DMA,
        ],
        compiler_params=pltpu.CompilerParams(vmem_limit_bytes=60 << 20),
        cost_estimate=pl.CostEstimate(flops=800000000, bytes_accessed=5000000, transcendentals=800000),
        name="first_layer",
    )(place, state, inv, bias, gain, qkv, o_weights, *fetched, gain_next)


def last_kernel(
    place_ref, is_first_ref,
    moved_ref, fresh_ref, bias_ref, gain_ref, qkv_ref, o_ref, chip_ref, first_ref, second_ref, swapped_ref,
    out_ref,
    slots_ref, packed_ref, state_ref, inv_ref, out_buf, slot_sems, sems, out_sems,
):
    rows, width = moved_ref.shape
    step = rows // PIECES
    blocks = [slice(p * step, (p + 1) * step) for p in range(PIECES)]

    def reads(source):
        return [
            pltpu.make_async_copy(source.at[block], state_ref.at[block], sems.at[p])
            for p, block in enumerate(blocks)
        ]

    slots = fetch_slots(
        lax.rem(place_ref[0], 2), chip_ref, first_ref, second_ref, swapped_ref, slots_ref, slot_sems
    )

    @pl.when(is_first_ref[0] == 1)
    def _():
        for copy in reads(fresh_ref):
            copy.start()

    @pl.when(is_first_ref[0] == 0)
    def _():
        for copy in reads(moved_ref):
            copy.start()

    for copy in slots:
        copy.wait()
    pack_slots(slots_ref, packed_ref, rows // RATE)
    for block, copy in zip(blocks, reads(moved_ref)):
        copy.wait()
        squares = None
        for head in range(HEADS):
            values = state_ref[block, head * DIM : (head + 1) * DIM].astype(f32)
            squares = values * values if squares is None else squares + values * values
        inverse = inverse_rms(jnp.sum(squares, axis=-1, keepdims=True), width)
        inv_ref[block] = jnp.broadcast_to(inverse, (step, DIM))
    inverse = inv_ref[...]
    bias = bias_ref[...]
    outs = []
    for group in range(HEADS // PACK):
        heads = range(group * PACK, (group + 1) * PACK)
        cols = [slice(head * DIM, (head + 1) * DIM) for head in heads]
        results = some_heads(
            [state_ref[:, c] for c in cols], inverse, [gain_ref[:, c] for c in cols],
            [qkv_ref[0, h] for h in heads], [qkv_ref[1, h] for h in heads], [qkv_ref[2, h] for h in heads],
            [o_ref[h] for h in heads], [packed_ref[:, c] for c in cols], bias,
        )
        for c, result in zip(cols, results):
            out_buf[:, c] = result
        block = slice(group * PACK * DIM, (group + 1) * PACK * DIM)
        out = pltpu.make_async_copy(out_buf.at[:, block], out_ref.at[:, block], out_sems.at[group])
        out.start()
        outs.append(out)
    for out in outs:
        out.wait()


def last_layer(place, is_first, moved, fresh, gain, bias, qkv, o_weights, fetched):
    rows, width = moved.shape
    return pl.pallas_call(
        last_kernel,
        out_shape=jax.ShapeDtypeStruct((rows, width), bf16),
        in_specs=[SMEM, SMEM, ANY, ANY, *[VMEM] * 4, *[ANY] * 4],
        out_specs=ANY,
        scratch_shapes=[
            pltpu.VMEM((SLOTS, PAD, width), bf16),
            pltpu.VMEM((KEYS - rows, width), f32),
            pltpu.VMEM((rows, width), bf16),
            pltpu.VMEM((rows, DIM), f32),
            pltpu.VMEM((rows, width), bf16),
            pltpu.SemaphoreType.DMA((SLOTS,)),
            pltpu.SemaphoreType.DMA((PIECES,)),
            pltpu.SemaphoreType.DMA((HEADS // PACK,)),
        ],
        compiler_params=pltpu.CompilerParams(vmem_limit_bytes=48 << 20),
        cost_estimate=pl.CostEstimate(flops=800000000, bytes_accessed=5000000, transcendentals=800000),
        name="last_layer",
    )(place, is_first, moved, fresh, bias, gain, qkv, o_weights, *fetched)


def shifted(value, axis, steps):
    count = lax.axis_size(axis)
    first, last = max(0, -steps), min(count, count - steps)
    return lax.ppermute(value, axis, [(source, source + steps) for source in range(first, last)])


def by_core(value, even_steps, odd_steps):
    chips = lax.axis_size("seq") // 2
    pairs = [(2 * c, 2 * (c + even_steps)) for c in range(chips - even_steps)]
    pairs += [(2 * c + 1, 2 * (c + odd_steps) + 1) for c in range(chips - odd_steps)]
    return lax.ppermute(value, "seq", pairs)


def fetch(panel, core, beside=None):
    count = lax.axis_size("seq")
    cores = [[chip, chip + 1] for chip in range(0, count, 2)]
    chip = lax.all_gather(panel, "seq", axis=0, axis_index_groups=cores)
    first = by_core(chip, 1, 4)
    second = by_core(chip, 2, 8)
    mine = jnp.stack(
        [
            lax.dynamic_index_in_dim(first, 1 - core, 0, keepdims=False),
            lax.dynamic_index_in_dim(second, 1 - core, 0, keepdims=False),
        ]
    )
    if beside is not None:
        mine, beside = lax.optimization_barrier((mine, beside))
    swapped = lax.all_gather(mine, "seq", axis=0, axis_index_groups=cores)
    return (chip, first, second, swapped) if beside is None else ((chip, first, second, swapped), beside)


def on_device(slabs, fresh, norm_gain, qkv_proj, o_proj, offsets):
    place = lax.axis_index("seq").astype(jnp.int32)
    section = lax.axis_index("section")
    core = lax.rem(place, 2)
    here = place.reshape(1)
    is_first = (section == 0).astype(jnp.int32)
    state, entering = slabs[0], fresh[0]
    gain, qkv, o_weights = norm_gain, qkv_proj[0], o_proj[0]

    panel, inv, ahead = norm_panel(offsets[0], state, gain)
    fetched, ahead = fetch(panel, core, shifted(ahead, "section", -1))
    own_panel, bias = entering_panel(here, is_first.reshape(1), offsets[0], entering, gain)
    output, panel_next = first_layer(
        here, state, inv, gain, bias, qkv, o_weights, fetched, ahead
    )
    moved_panel = shifted(panel_next, "section", 1)
    moved = shifted(output, "section", 1)
    panel = jnp.where(is_first == 1, own_panel, moved_panel)
    fetched = lax.fori_loop(
        0, 1 + jnp.minimum(offsets[0, 0], 0), lambda _, previous: fetch(panel, core), fetched
    )
    result = last_layer(here, is_first.reshape(1), moved, entering, gain, bias, qkv, o_weights, fetched)
    return result[None]


def solution(mesh):
    in_specs = (
        P("section", "seq", None),
        P(None, "seq", None),
        P("section", None),
        P("section", None, None, None, None),
        P("section", None, None, None),
        P("section", None),
    )
    out_specs = P("section", "seq", None)
    return jax.shard_map(
        on_device, mesh=mesh, in_specs=in_specs, out_specs=out_specs, check_vma=False
    )
```

```python
import functools
import math

import jax
import jax.numpy as jnp
from jax import lax
from jax.experimental import pallas as pl
from jax.experimental.pallas import tpu as pltpu
from jax.sharding import PartitionSpec as P

RATE = 16
HEADS = 16
DIM = 128
PACK = 8
SLOTS = 5
KEYS = 256
PIECES = 4
PAD = 16

eps = 1e-06
neg_big = -1e30
f32 = jnp.float32
bf16 = jnp.bfloat16

SMEM = pl.BlockSpec(memory_space=pltpu.SMEM)
VMEM = pl.BlockSpec(memory_space=pltpu.VMEM)
ANY = pl.BlockSpec(memory_space=pl.ANY)


def inverse_rms(squares, width):
    return lax.rsqrt(squares * (1.0 / width) + eps)


def pick_panel(wide_ref, inv_ref, gain_ref, offset_of, panel_ref):
    count = wide_ref.shape[1] // RATE
    for head in range(HEADS):
        cols = slice(head * DIM, (head + 1) * DIM)
        where = pl.ds(offset_of(head), count, stride=RATE)
        picked = wide_ref[head, where, :] * inv_ref[where, :] * gain_ref[:, cols].astype(f32)
        panel_ref[:, cols] = jnp.concatenate(
            [picked, jnp.zeros((PAD - count, DIM), f32)], axis=0
        ).astype(bf16)


def norm_kernel(offsets_ref, state_ref, gain_ref, panel_ref, inv_ref, ahead_ref, wide_ref):
    width = state_ref.shape[1]
    ahead_ref[:, :width] = gain_ref[...]
    lane = lax.broadcasted_iota(jnp.int32, (1, DIM), 1)
    phases = jnp.zeros((1, DIM), jnp.int32)
    for head in range(HEADS):
        phases = jnp.where(lane == head, offsets_ref[head], phases)
    ahead_ref[:, width:] = phases.astype(f32).astype(bf16)
    squares = None
    for head in range(HEADS):
        cols = slice(head * DIM, (head + 1) * DIM)
        values = state_ref[:, cols].astype(f32)
        wide_ref[head] = values
        squares = values * values if squares is None else squares + values * values
    inverse = inverse_rms(jnp.sum(squares, axis=-1, keepdims=True), width)
    inv_ref[...] = jnp.broadcast_to(inverse, inv_ref.shape)
    pick_panel(wide_ref, inv_ref, gain_ref, lambda head: offsets_ref[head], panel_ref)


def norm_panel(offsets, state, gain):
    rows, width = state.shape
    return pl.pallas_call(
        norm_kernel,
        out_shape=(
            jax.ShapeDtypeStruct((PAD, width), bf16),
            jax.ShapeDtypeStruct((rows, DIM), f32),
            jax.ShapeDtypeStruct((1, width + DIM), bf16),
        ),
        in_specs=[SMEM, VMEM, VMEM],
        out_specs=(VMEM, VMEM, VMEM),
        scratch_shapes=[pltpu.VMEM((HEADS, rows, DIM), f32)],
        cost_estimate=pl.CostEstimate(flops=2000000, bytes_accessed=1000000, transcendentals=0),
        name="norm_panel",
    )(offsets, state, gain)


def pack_panels(core, chip_ref, first_ref, second_ref, swapped_ref, packed_ref, count):
    width = packed_ref.shape[1]
    other = 1 - core
    slots = [
        jnp.where(core == 0, first_ref[1], chip_ref[0]),
        first_ref[core],
        second_ref[core],
        swapped_ref[other, 0],
        swapped_ref[other, 1],
    ]
    for slot, panel in enumerate(slots):
        packed_ref[slot * count : (slot + 1) * count, :] = panel[:count].astype(f32)
    packed_ref[SLOTS * count :, :] = jnp.zeros((packed_ref.shape[0] - SLOTS * count, width), f32)


def fetch_slots(core, chip_ref, first_ref, second_ref, swapped_ref, slots_ref, sems):
    other = 1 - core
    sources = [first_ref.at[core], second_ref.at[core], swapped_ref.at[other, 0], swapped_ref.at[other, 1]]
    copies = [
        pltpu.make_async_copy(source, slots_ref.at[1 + slot], sems.at[1 + slot])
        for slot, source in enumerate(sources)
    ]
    for copy in copies:
        copy.start()

    @pl.when(core == 0)
    def _():
        pltpu.make_async_copy(first_ref.at[1], slots_ref.at[0], sems.at[0]).start()

    @pl.when(core == 1)
    def _():
        pltpu.make_async_copy(chip_ref.at[0], slots_ref.at[0], sems.at[0]).start()

    return [pltpu.make_async_copy(chip_ref.at[0], slots_ref.at[0], sems.at[0]), *copies]


def pack_slots(slots_ref, packed_ref, count):
    width = packed_ref.shape[1]
    for slot in range(SLOTS):
        packed_ref[slot * count : (slot + 1) * count, :] = slots_ref[slot][:count].astype(f32)
    packed_ref[SLOTS * count :, :] = jnp.zeros((packed_ref.shape[0] - SLOTS * count, width), f32)


def write_bias(place, bias_ref, count):
    rows, keys = bias_ref.shape
    core = lax.rem(place, 2)
    even, odd = (1, 2, 4, 8, 16), (1, 8, 16, 2, 4)
    row = lax.broadcasted_iota(jnp.int32, (rows, keys), 0)
    col = lax.broadcasted_iota(jnp.int32, (rows, keys), 1)
    allowed = (col < rows) & (col <= row)
    for slot in range(SLOTS):
        distance = jnp.where(core == 0, even[slot], odd[slot])
        start = jnp.where(place >= distance, rows + slot * count, keys)
        allowed = allowed | ((col >= start) & (col < rows + (slot + 1) * count))
    bias_ref[...] = jnp.where(allowed, 0.0, neg_big).astype(bf16)


def entering_kernel(place_ref, is_first_ref, offsets_ref, fresh_ref, gain_ref, panel_ref, bias_ref, state_ref, wide_ref, inv_ref, sem):
    write_bias(place_ref[0], bias_ref, wide_ref.shape[1] // RATE)

    @pl.when(is_first_ref[0] == 1)
    def _():
        copy = pltpu.make_async_copy(fresh_ref, state_ref, sem)
        copy.start()
        copy.wait()
        squares = None
        for head in range(HEADS):
            values = state_ref[:, head * DIM : (head + 1) * DIM].astype(f32)
            wide_ref[head] = values
            squares = values * values if squares is None else squares + values * values
        inverse = inverse_rms(jnp.sum(squares, axis=-1, keepdims=True), HEADS * DIM)
        inv_ref[...] = jnp.broadcast_to(inverse, inv_ref.shape)
        pick_panel(wide_ref, inv_ref, gain_ref, lambda head: offsets_ref[head], panel_ref)

    @pl.when(is_first_ref[0] == 0)
    def _():
        panel_ref[...] = jnp.zeros(panel_ref.shape, panel_ref.dtype)


def entering_panel(place, is_first, offsets, fresh, gain):
    rows, width = fresh.shape
    return pl.pallas_call(
        entering_kernel,
        out_shape=(
            jax.ShapeDtypeStruct((PAD, width), bf16),
            jax.ShapeDtypeStruct((rows, KEYS), bf16),
        ),
        in_specs=[SMEM, SMEM, SMEM, ANY, VMEM],
        out_specs=(VMEM, VMEM),
        scratch_shapes=[
            pltpu.VMEM((rows, width), bf16),
            pltpu.VMEM((HEADS, rows, DIM), f32),
            pltpu.VMEM((rows, DIM), f32),
            pltpu.SemaphoreType.DMA,
        ],
        compiler_params=pltpu.CompilerParams(vmem_limit_bytes=60 << 20),
        cost_estimate=pl.CostEstimate(flops=2000000, bytes_accessed=1000000, transcendentals=0),
        name="entering_panel",
    )(place, is_first, offsets, fresh, gain)


def some_heads(states, inverse, gains, queries, keys, values, outs, panels, bias):
    scale = math.log2(math.e) / math.sqrt(DIM)
    wide = [state.astype(f32) for state in states]
    normed = [(w * inverse * gain.astype(f32)).astype(bf16) for w, gain in zip(wide, gains)]
    both = [jnp.concatenate([n, panel.astype(bf16)], axis=0) for n, panel in zip(normed, panels)]
    query = [jnp.dot(n, w, preferred_element_type=f32).astype(bf16) for n, w in zip(normed, queries)]
    pair = [
        jnp.dot(rows, jnp.concatenate([k, v], axis=1), preferred_element_type=f32).astype(bf16)
        for rows, k, v in zip(both, keys, values)
    ]
    scores = [
        lax.dot_general(q, p[:, :DIM], (((1,), (1,)), ((), ())), preferred_element_type=f32)
        for q, p in zip(query, pair)
    ]
    scores = [s * scale + bias for s in scores]
    expo = [jnp.exp2(s - jnp.max(s, axis=-1, keepdims=True)) for s in scores]
    total = [jnp.sum(e, axis=-1, keepdims=True) for e in expo]
    summed = [
        jnp.dot(e.astype(bf16), p[:, DIM:], preferred_element_type=f32) for e, p in zip(expo, pair)
    ]
    attended = [(m * (1.0 / t)).astype(bf16) for m, t in zip(summed, total)]
    mixed = [jnp.dot(a, w, preferred_element_type=f32) for a, w in zip(attended, outs)]
    return [(w + m).astype(bf16) for w, m in zip(wide, mixed)]


def first_kernel(
    place_ref,
    state_ref, inv_ref, bias_ref, gain_ref, qkv_ref, o_ref, chip_ref, first_ref, second_ref, swapped_ref, gain_next_ref,
    out_ref, panel_ref,
    packed_ref, wide_ref, squares_ref, inv_next_ref, phases_ref, phases_smem, sem,
):
    step = pl.program_id(0)
    rows = state_ref.shape[0]
    count = rows // RATE

    @pl.when(step == 0)
    def _():
        phases_ref[...] = gain_next_ref[:, HEADS * DIM :].astype(f32).astype(jnp.int32)
        pltpu.make_async_copy(phases_ref, phases_smem, sem).start()
        pack_panels(
            lax.rem(place_ref[0], 2), chip_ref, first_ref, second_ref, swapped_ref, packed_ref, count
        )

    inverse, bias = inv_ref[...], bias_ref[...].astype(f32)
    squares = jnp.zeros((rows, DIM), f32)
    local_cols = [slice(local * DIM, (local + 1) * DIM) for local in range(PACK)]
    there = [pl.ds(pl.multiple_of((step * PACK + local) * DIM, DIM), DIM) for local in range(PACK)]
    results = some_heads(
        [state_ref[:, cols] for cols in local_cols], inverse, [gain_ref[:, cols] for cols in local_cols],
        [qkv_ref[0, i] for i in range(PACK)], [qkv_ref[1, i] for i in range(PACK)], [qkv_ref[2, i] for i in range(PACK)],
        [o_ref[i] for i in range(PACK)], [packed_ref[:, at] for at in there], bias,
    )
    for local, result in enumerate(results):
        out_ref[:, local_cols[local]] = result
        values = result.astype(f32)
        wide_ref[step * PACK + local] = values
        squares = squares + values * values
    squares_ref[...] = jnp.where(step == 0, squares, squares_ref[...] + squares)

    @pl.when(step == pl.num_programs(0) - 1)
    def _():
        total = jnp.sum(squares_ref[...], axis=-1, keepdims=True)
        inv_next_ref[...] = jnp.broadcast_to(inverse_rms(total, HEADS * DIM), inv_next_ref.shape)
        pltpu.make_async_copy(phases_ref, phases_smem, sem).wait()
        pick_panel(wide_ref, inv_next_ref, gain_next_ref, lambda head: phases_smem[0, head], panel_ref)


def attention_specs(rows, width):
    return [
        pl.BlockSpec((1, PACK * DIM), lambda i: (0, i)),
        pl.BlockSpec((3, PACK, DIM, DIM), lambda i: (0, i, 0, 0)),
        pl.BlockSpec((PACK, DIM, DIM), lambda i: (i, 0, 0)),
        pl.BlockSpec((2, PAD, width), lambda i: (0, 0, 0)),
        pl.BlockSpec((2, PAD, width), lambda i: (0, 0, 0)),
        pl.BlockSpec((2, PAD, width), lambda i: (0, 0, 0)),
        pl.BlockSpec((2, 2, PAD, width), lambda i: (0, 0, 0, 0)),
    ]


def first_layer(place, state, inv, gain, bias, qkv, o_weights, fetched, gain_next):
    rows, width = state.shape
    return pl.pallas_call(
        first_kernel,
        grid=(HEADS // PACK,),
        out_shape=(
            jax.ShapeDtypeStruct((rows, width), bf16),
            jax.ShapeDtypeStruct((PAD, width), bf16),
        ),
        in_specs=[
            SMEM,
            pl.BlockSpec((rows, PACK * DIM), lambda i: (0, i)),
            pl.BlockSpec((rows, DIM), lambda i: (0, 0)),
            pl.BlockSpec((rows, KEYS), lambda i: (0, 0)),
            *attention_specs(rows, width),
            pl.BlockSpec((1, width + DIM), lambda i: (0, 0)),
        ],
        out_specs=(
            pl.BlockSpec((rows, PACK * DIM), lambda i: (0, i)),
            pl.BlockSpec((PAD, width), lambda i: (0, 0)),
        ),
        scratch_shapes=[
            pltpu.VMEM((KEYS - rows, width), f32),
            pltpu.VMEM((HEADS, rows, DIM), f32),
            pltpu.VMEM((rows, DIM), f32),
            pltpu.VMEM((rows, DIM), f32),
            pltpu.VMEM((1, DIM), jnp.int32),
            pltpu.SMEM((1, DIM), jnp.int32),
            pltpu.SemaphoreType.DMA,
        ],
        compiler_params=pltpu.CompilerParams(vmem_limit_bytes=60 << 20),
        cost_estimate=pl.CostEstimate(flops=800000000, bytes_accessed=5000000, transcendentals=800000),
        name="first_layer",
    )(place, state, inv, bias, gain, qkv, o_weights, *fetched, gain_next)


def last_kernel(
    place_ref, is_first_ref,
    moved_ref, fresh_ref, bias_ref, gain_ref, qkv_ref, o_ref, chip_ref, first_ref, second_ref, swapped_ref,
    out_ref,
    slots_ref, packed_ref, state_ref, inv_ref, out_buf, slot_sems, sems, out_sems,
):
    rows, width = moved_ref.shape
    step = rows // PIECES
    blocks = [slice(p * step, (p + 1) * step) for p in range(PIECES)]

    def reads(source):
        return [
            pltpu.make_async_copy(source.at[block], state_ref.at[block], sems.at[p])
            for p, block in enumerate(blocks)
        ]

    slots = fetch_slots(
        lax.rem(place_ref[0], 2), chip_ref, first_ref, second_ref, swapped_ref, slots_ref, slot_sems
    )

    @pl.when(is_first_ref[0] == 1)
    def _():
        for copy in reads(fresh_ref):
            copy.start()

    @pl.when(is_first_ref[0] == 0)
    def _():
        for copy in reads(moved_ref):
            copy.start()

    for copy in slots:
        copy.wait()
    pack_slots(slots_ref, packed_ref, rows // RATE)
    for block, copy in zip(blocks, reads(moved_ref)):
        copy.wait()
        squares = None
        for head in range(HEADS):
            values = state_ref[block, head * DIM : (head + 1) * DIM].astype(f32)
            squares = values * values if squares is None else squares + values * values
        inverse = inverse_rms(jnp.sum(squares, axis=-1, keepdims=True), width)
        inv_ref[block] = jnp.broadcast_to(inverse, (step, DIM))
    inverse = inv_ref[...]
    bias = bias_ref[...].astype(f32)
    outs = []
    for group in range(HEADS // PACK):
        heads = range(group * PACK, (group + 1) * PACK)
        cols = [slice(head * DIM, (head + 1) * DIM) for head in heads]
        results = some_heads(
            [state_ref[:, c] for c in cols], inverse, [gain_ref[:, c] for c in cols],
            [qkv_ref[0, h] for h in heads], [qkv_ref[1, h] for h in heads], [qkv_ref[2, h] for h in heads],
            [o_ref[h] for h in heads], [packed_ref[:, c] for c in cols], bias,
        )
        for c, result in zip(cols, results):
            out_buf[:, c] = result
        block = slice(group * PACK * DIM, (group + 1) * PACK * DIM)
        out = pltpu.make_async_copy(out_buf.at[:, block], out_ref.at[:, block], out_sems.at[group])
        out.start()
        outs.append(out)
    for out in outs:
        out.wait()


def last_layer(place, is_first, moved, fresh, gain, bias, qkv, o_weights, fetched):
    rows, width = moved.shape
    return pl.pallas_call(
        last_kernel,
        out_shape=jax.ShapeDtypeStruct((rows, width), bf16),
        in_specs=[SMEM, SMEM, ANY, ANY, *[VMEM] * 4, *[ANY] * 4],
        out_specs=ANY,
        scratch_shapes=[
            pltpu.VMEM((SLOTS, PAD, width), bf16),
            pltpu.VMEM((KEYS - rows, width), f32),
            pltpu.VMEM((rows, width), bf16),
            pltpu.VMEM((rows, DIM), f32),
            pltpu.VMEM((rows, width), bf16),
            pltpu.SemaphoreType.DMA((SLOTS,)),
            pltpu.SemaphoreType.DMA((PIECES,)),
            pltpu.SemaphoreType.DMA((HEADS // PACK,)),
        ],
        compiler_params=pltpu.CompilerParams(vmem_limit_bytes=48 << 20),
        cost_estimate=pl.CostEstimate(flops=800000000, bytes_accessed=5000000, transcendentals=800000),
        name="last_layer",
    )(place, is_first, moved, fresh, bias, gain, qkv, o_weights, *fetched)


def shifted(value, axis, steps):
    count = lax.axis_size(axis)
    first, last = max(0, -steps), min(count, count - steps)
    return lax.ppermute(value, axis, [(source, source + steps) for source in range(first, last)])


def by_core(value, even_steps, odd_steps):
    chips = lax.axis_size("seq") // 2
    pairs = [(2 * c, 2 * (c + even_steps)) for c in range(chips - even_steps)]
    pairs += [(2 * c + 1, 2 * (c + odd_steps) + 1) for c in range(chips - odd_steps)]
    return lax.ppermute(value, "seq", pairs)


def fetch(panel, core, beside=None):
    count = lax.axis_size("seq")
    cores = [[chip, chip + 1] for chip in range(0, count, 2)]
    chip = lax.all_gather(panel, "seq", axis=0, axis_index_groups=cores)
    first = by_core(chip, 1, 4)
    second = by_core(chip, 2, 8)
    mine = jnp.stack(
        [
            lax.dynamic_index_in_dim(first, 1 - core, 0, keepdims=False),
            lax.dynamic_index_in_dim(second, 1 - core, 0, keepdims=False),
        ]
    )
    if beside is not None:
        mine, beside = lax.optimization_barrier((mine, beside))
    swapped = lax.all_gather(mine, "seq", axis=0, axis_index_groups=cores)
    return (chip, first, second, swapped) if beside is None else ((chip, first, second, swapped), beside)


def on_device(slabs, fresh, norm_gain, qkv_proj, o_proj, offsets):
    place = lax.axis_index("seq").astype(jnp.int32)
    section = lax.axis_index("section")
    core = lax.rem(place, 2)
    here = place.reshape(1)
    is_first = (section == 0).astype(jnp.int32)
    state, entering = slabs[0], fresh[0]
    gain, qkv, o_weights = norm_gain, qkv_proj[0], o_proj[0]

    panel, inv, ahead = norm_panel(offsets[0], state, gain)
    fetched, ahead = fetch(panel, core, shifted(ahead, "section", -1))
    own_panel, bias = entering_panel(here, is_first.reshape(1), offsets[0], entering, gain)
    output, panel_next = first_layer(
        here, state, inv, gain, bias, qkv, o_weights, fetched, ahead
    )
    moved_panel = shifted(panel_next, "section", 1)
    moved = shifted(output, "section", 1)
    panel = jnp.where(is_first == 1, own_panel, moved_panel)
    fetched = lax.fori_loop(
        0, 1 + jnp.minimum(offsets[0, 0], 0), lambda _, previous: fetch(panel, core), fetched
    )
    result = last_layer(here, is_first.reshape(1), moved, entering, gain, bias, qkv, o_weights, fetched)
    return result[None]


def solution(mesh):
    in_specs = (
        P("section", "seq", None),
        P(None, "seq", None),
        P("section", None),
        P("section", None, None, None, None),
        P("section", None, None, None),
        P("section", None),
    )
    out_specs = P("section", "seq", None)
    return jax.shard_map(
        on_device, mesh=mesh, in_specs=in_specs, out_specs=out_specs, check_vma=False
    )
```
